32 devices in a mesh: wide: 8 (over z, x), narrow: 4 (over y, core).
Axes of the slice: x: 2, y: 2, z: 4, core: 2. Of those that a mesh axis runs over, the one named last changes fastest.
Arguments:
- tokens: bfloat16 [32, 512, 1120], P('wide', 'narrow'), may hold values from -6 to 6
- lengths: int32 [32], P('wide'), may hold values from 64 to 512, as said below
- norm1_gain: float32 [1120], replicated, may hold values from 0.1 to 1.9
- norm1_bias: float32 [1120], replicated, may hold values from -3 to 3
- w_qkv: bfloat16 [1120, 3, 1120], replicated, may hold values from -0.25 to 0.25
- w_out: bfloat16 [1120, 1120], replicated, may hold values from -1 to 1
- norm2_gain: float32 [1120], replicated, may hold values from 0.1 to 1.9
- norm2_bias: float32 [1120], replicated, may hold values from -3 to 3
- w_up: bfloat16 [1120, 4480], replicated, may hold values from -0.1875 to 0.1875
- bias_up: float32 [4480], replicated, may hold values from -3 to 3
- w_down: bfloat16 [4480, 1120], replicated, may hold values from -0.09375 to 0.09375
- bias_down: float32 [1120], replicated, may hold values from -3 to 3
- cotangent: bfloat16 [32, 512, 1120], P('wide', 'narrow'), may hold values from -6 to 6
Outputs:
- output: bfloat16 [32, 512, 1120], P('wide', 'narrow')
- input_grad: float32 [32, 512, 1120], P('wide', 'narrow')
- grad_norm1_gain: float32 [1120], P('narrow')
- grad_norm1_bias: float32 [1120], P('narrow')
- grad_w_qkv: float32 [1120, 3, 1120], P(None, None, 'narrow')
- grad_w_out: float32 [1120, 1120], P('narrow')
- grad_norm2_gain: float32 [1120], P('narrow')
- grad_norm2_bias: float32 [1120], P('narrow')
- grad_w_up: float32 [1120, 4480], P(None, 'narrow')
- grad_bias_up: float32 [4480], P('narrow')
- grad_w_down: float32 [4480, 1120], P('narrow')
- grad_bias_down: float32 [1120], P('narrow')
The draws below stay inside these ranges and needn't reach their ends.
Inputs may be any that keep to these rules, and one draw needn't show every extreme that they name: In every aligned block of 4 cells (the cells of one index of wide) exactly one cell, drawn from the seed, has length 512; in one block, drawn from the seed, another cell has length 64; the other lengths follow a heavy tail and are mostly short.
All inputs are finite; a program needn't handle non-finite values.
Results may differ from the reference program's by a relative error of at most 0.015.
The reference program's roundings to bfloat16 on the way count: a program that leaves them out, or rounds other values in their place, can miss the bound.
Values may be sent and summed in bfloat16 or wider, within the bound.
A program may use at most 192 MiB of HBM per device.

```python
import jax
import jax.numpy as jnp
from jax import lax

D = 1120
HEADS = 20
HD = 56
FF = 4480
CELLS_DEV = 4
SEQ = 512
CELLS = 32


def draw_lengths(key, part):
    key = jax.random.fold_in(key, 7)
    key_tail, key_slot, key_group = jax.random.split(key, 3)
    factors = jax.random.randint(key_tail, (3, CELLS), 0, 64)
    product = factors[0] * factors[1] * factors[2]
    shortest = SEQ // 8
    tail = shortest + (SEQ - shortest) * product // 262144
    group_count = CELLS // CELLS_DEV
    slots = jax.random.randint(key_slot, (group_count,), 0, CELLS_DEV)
    cell_index = jnp.arange(CELLS)
    full_slot = jnp.repeat(slots, CELLS_DEV, total_repeat_length=CELLS)
    slot_in_group = cell_index % CELLS_DEV
    chosen = jax.random.randint(key_group, (), 0, group_count)
    short_cell = chosen * CELLS_DEV + (slots[chosen] + 1) % CELLS_DEV
    result = jnp.where(cell_index == short_cell, shortest, tail)
    result = jnp.where(slot_in_group == full_slot, SEQ, result)
    return result.astype(jnp.int32)


def block_levels(rng, extent, cuts, smallest, high):
    def one(axis_at, shards_of):
        steps = jax.random.uniform(jax.random.fold_in(jax.random.fold_in(rng, 6), axis_at), (shards_of,), jnp.float32, smallest / len(cuts), high / len(cuts))
        return jnp.repeat(jnp.exp(steps), extent[axis_at] // shards_of).reshape((-1,) + (1,) * (len(extent) - axis_at - 1))

    loudness = one(*cuts[0])
    for cut in cuts[1:]:
        loudness = loudness * one(*cut)
    return loudness


def bell_draw(stream_key, dims, deviation, limit, pieces=(), held_as=jnp.bfloat16):
    level = block_levels(stream_key, dims, pieces, -0.22, 0.18) if pieces else 1.0
    values = jax.random.normal(stream_key, dims, jnp.float32) * deviation * level
    return jnp.minimum(jnp.maximum(values, -limit), limit).astype(held_as)


def setup_inputs(seed: int = 0) -> dict:
    key_of = jax.random.split(jax.random.key(seed), 14)
    return {
        "tokens": bell_draw(key_of[0], (CELLS, SEQ, D), 1.0, 6.0, ((0, 8), (1, 4))),
        "lengths": draw_lengths(jax.random.fold_in(key_of[13], 71), 0),
        "norm1_gain": jnp.clip(1.0 + 0.18 * jax.random.normal(key_of[2], (D,), jnp.float32), 0.1, 1.9),
        "norm1_bias": bell_draw(key_of[3], (D,), 0.5, 3.0, (), jnp.float32),
        "w_qkv": bell_draw(key_of[4], (D, 3, D), (D // 2) ** -0.5, 0.25),
        "w_out": bell_draw(key_of[5], (D, D), (max(D // 32, 8)) ** -0.5, 1.0),
        "norm2_gain": jnp.clip(1.0 + 0.18 * jax.random.normal(key_of[6], (D,), jnp.float32), 0.1, 1.9),
        "norm2_bias": bell_draw(key_of[7], (D,), 0.5, 3.0, (), jnp.float32),
        "w_up": bell_draw(key_of[8], (D, FF), D ** -0.5, 0.1875),
        "bias_up": bell_draw(key_of[9], (FF,), 0.5, 3.0, (), jnp.float32),
        "w_down": bell_draw(key_of[10], (FF, D), FF ** -0.5, 0.09375),
        "bias_down": bell_draw(key_of[11], (D,), 0.5, 3.0, (), jnp.float32),
        "cotangent": bell_draw(key_of[12], (CELLS, SEQ, D), 1.0, 6.0, ((0, 8), (1, 4))),
    }


@jax.custom_vjp
def low(v):
    return lax.optimization_barrier(v.astype(jnp.bfloat16)).astype(jnp.float32)

@jax.custom_vjp
def low_back(v):
    return v

def low_keep(v):
    return (low(v), None)

def low_pass(kept, grad):
    return (grad,)

def back_keep(v):
    return (v, None)

def back_low(kept, grad):
    return (low(grad),)
low.defvjp(low_keep, low_pass)
low_back.defvjp(back_keep, back_low)

def layer_norm(values, gain, shift):
    mean_value = lax.optimization_barrier(jnp.mean(values, axis=-1, keepdims=True))
    centred = values - mean_value
    variance = lax.optimization_barrier(jnp.mean(centred * centred, axis=-1, keepdims=True))
    return centred * lax.rsqrt(variance + 1e-05) * gain + shift

def cell_forward(cell_tokens, length, weights):
    gain_one, bias_one, w_qkv, w_out, gain_two, bias_two, w_up, bias_up, w_down, bias_down = weights
    highest = lax.Precision.HIGHEST
    hidden1 = low(layer_norm(cell_tokens, gain_one, bias_one))
    projected = low(low_back(jnp.einsum('pd,dke->pke', hidden1, w_qkv, precision=highest)))
    query = projected[:, 0].reshape(SEQ, HEADS, HD)
    keys = projected[:, 1].reshape(SEQ, HEADS, HD)
    values = projected[:, 2].reshape(SEQ, HEADS, HD)
    raw = low_back(jnp.einsum('qhe,khe->hqk', query, keys, precision=highest))
    scores = raw * HD ** (-0.5)
    positions = jnp.arange(SEQ)
    allowed = (positions[None, :] <= positions[:, None]) & (positions[None, :] < length)
    scores = jnp.where(allowed[None], scores, jnp.float32(-1e+30))
    probs = jax.nn.softmax(scores, axis=-1)
    mixed = jnp.einsum('hqk,khe->qhe', low(probs), values, precision=highest).reshape(SEQ, D)
    attended = low(low_back(mixed))
    after = cell_tokens + low_back(jnp.dot(attended, w_out, precision=highest))
    hidden2 = low(layer_norm(after, gain_two, bias_two))
    upper = low_back(jnp.dot(hidden2, w_up, precision=highest) + bias_up)
    activated = low(jax.nn.gelu(upper, approximate=True))
    return after + jnp.dot(activated, w_down, precision=highest) + bias_down

def reference(tokens, lengths, norm1_gain, norm1_bias, w_qkv, w_out, norm2_gain, norm2_bias, w_up, bias_up, w_down, bias_down, cotangent):
    floats = [item.astype(jnp.float32) for item in (tokens, norm1_gain, norm1_bias, w_qkv, w_out, norm2_gain, norm2_bias, w_up, bias_up, w_down, bias_down)]

    def forward(tokens_float, *weights):

        def one_cell(item):
            return cell_forward(item[0], item[1], weights)
        return lax.map(jax.checkpoint(one_cell), (tokens_float, lengths))
    output, pullback = jax.vjp(forward, *floats)
    grads = pullback(cotangent.astype(jnp.float32))
    return (output.astype(jnp.bfloat16), grads[0], grads[1], grads[2], grads[3], grads[4], grads[5], grads[6], grads[7], grads[8], grads[9], grads[10])
```

```python
import functools
import types

import jax
import jax.numpy as jnp
from jax import lax
from jax.experimental import pallas as pl
from jax.experimental.pallas import tpu as pltpu
from jax.sharding import PartitionSpec as P

HD = 56
SCALE = HD**-0.5
F32, BF16 = jnp.float32, jnp.bfloat16
MESH = pl.DeviceIdType.MESH
VMEM_LIMIT = 62 * 1024 * 1024
LINE, PAIR = 4, 2
BLOCK = LINE * PAIR
SLOTS, STATES, STATES_A = 4, 11, 8
CORE, CY, CA, CB, CC, CX, AX, AY, A1, A2, A3, AG, GATHER = range(13)
CHANNELS = GATHER + 6


def dot(a, b, dims):
    return lax.dot_general(a, b, (dims, ((), ())), preferred_element_type=F32)


NN, NT, TN = ((1,), (0,)), ((1,), (1,)), ((0,), (0,))


def head_mask(h, start, size):
    lane = start + lax.broadcasted_iota(jnp.int32, (1, size), 1)
    return (lane >= h * HD) & (lane < h * HD + HD)


class Reducer:
    hops = 9

    def __init__(self, rows_c, rows_a, width):
        self.rows_c, self.rows_a, self.width = rows_c, rows_a, width
        self.rows = rows_c + rows_a
        self.shard, self.half = rows_c // LINE, rows_a // 2

    def scratch(self):
        c, a, q, h, d = self.rows_c, self.rows_a, self.shard, self.half, self.width
        buffers = dict(
            own=(2, self.rows, d),
            core_in=(SLOTS, 2, self.rows, d),
            cy_out=(2, c, d),
            cy_in=(SLOTS, c, d),
            c_state=(STATES, c, d),
            ca_in=(SLOTS, 3 * q, d),
            cb_in=(SLOTS, 2 * q, d),
            cc_in=(SLOTS, q, d),
            cx_in=(SLOTS, q, d),
            ax_out=(2, 2, h, d),
            ax_keep=(2, 2, h, d),
            ax_in=(SLOTS, 2, h, d),
            ay_out=(2, h, d),
            ay_in=(SLOTS, h, d),
            a_sum=(4, h, d),
            a1_in=(SLOTS, h, d),
            a2_in=(SLOTS, h, d),
            a_state=(STATES_A, 2, h, d),
        )
        result = {name: pltpu.VMEM(shape, BF16) for name, shape in buffers.items()}
        result.update(
            net_send=pltpu.SemaphoreType.DMA((CHANNELS, SLOTS)),
            net_recv=pltpu.SemaphoreType.DMA((CHANNELS, SLOTS)),
            load=pltpu.SemaphoreType.DMA((2,)),
            c_store=pltpu.SemaphoreType.DMA((2,)),
            a_store=pltpu.SemaphoreType.DMA((2,)),
        )
        return result

    def bind(self, part_ref, out_ref, refs):
        self.part_ref, self.out_ref, self.refs = part_ref, out_ref, refs
        wide, narrow = lax.axis_index("wide"), lax.axis_index("narrow")
        self.wide, self.narrow = wide, narrow
        self.z, self.x = lax.rem(wide, BLOCK) // PAIR, lax.rem(wide, PAIR)
        self.y, self.core = narrow // 2, lax.rem(narrow, 2)
        flip = lambda index, bit: index + 1 - 2 * bit
        self.at_core = (wide, flip(narrow, self.core))
        self.at_y = (wide, narrow + 2 - 4 * self.y)
        self.at_cross = (wide, flip(narrow, self.core) + 2 - 4 * self.y)
        self.at_x = (flip(wide, self.x), narrow)
        self.at_up = (wide + PAIR, narrow)
        self.at_down = (wide - PAIR, narrow)
        self.rounds = out_ref.shape[0] // self.rows

    def barrier(self):
        z = self.z
        barrier = pltpu.get_barrier_semaphore()

        def greet(target):
            pl.semaphore_signal(barrier, inc=1, device_id=target, device_id_type=MESH)

        for target in (self.at_core, self.at_y, self.at_cross, self.at_x):
            greet(target)
        pl.when(z < LINE - 1)(lambda: greet(self.at_up))
        pl.when(z > 0)(lambda: greet(self.at_down))
        edge = (z == 0) | (z == LINE - 1)
        pl.when(edge)(lambda: pl.semaphore_wait(barrier, 5))
        pl.when(~edge)(lambda: pl.semaphore_wait(barrier, 6))

    def copy(self, channel, k, source, target, device):
        slot = lax.rem(k, SLOTS)
        return pltpu.make_async_remote_copy(
            src_ref=source,
            dst_ref=target,
            send_sem=self.refs.net_send.at[channel, slot],
            recv_sem=self.refs.net_recv.at[channel, slot],
            device_id=device,
            device_id_type=MESH,
        )


    def load(self, k):
        r = self.refs
        return pltpu.make_async_copy(
            self.part_ref.at[:, self.core, pl.ds(k * self.rows, self.rows)],
            r.own,
            r.load.at[lax.rem(k, 2)],
        )

    def core_hop(self, k):
        return self.copy(
            CORE,
            k,
            self.part_ref.at[:, 1 - self.core, pl.ds(k * self.rows, self.rows)],
            self.refs.core_in.at[lax.rem(k, SLOTS)],
            self.at_core,
        )

    def slotted(self, channel, k, source, device):
        r = self.refs
        arrivals = {CY: r.cy_in, CA: r.ca_in, CB: r.cb_in, CC: r.cc_in, CX: r.cx_in}
        arrivals.update({AX: r.ax_in, AY: r.ay_in, A1: r.a1_in, A2: r.a2_in})
        return self.copy(channel, k, source, arrivals[channel].at[lax.rem(k, SLOTS)], device)

    def c_rows(self, k, first, count):
        return self.refs.c_state.at[
            lax.rem(k, STATES), pl.ds(pl.multiple_of(first * self.shard, self.shard), count * self.shard)
        ]

    def line_hops(self, k):
        z, up, down = self.z, self.at_up, self.at_down
        hops = []
        for name, count, up_from in ((CA, 3, 0), (CB, 2, 1), (CC, 1, 2)):
            down_from = LINE - 1 - up_from
            hops.append(
                (
                    name,
                    [
                        (z == up_from, self.slotted(name, k, self.c_rows(k, LINE - count, count), up)),
                        (z == down_from, self.slotted(name, k, self.c_rows(k, 0, count), down)),
                    ],
                    [(z == up_from + 1, LINE - count), (z == down_from - 1, 0)],
                    count,
                )
            )
        return hops

    def gather_hops(self, k, distance):
        z = self.z
        channel = GATHER + 2 * distance
        low, high = jnp.maximum(z - distance, 0), jnp.minimum(z + distance, LINE - 1)
        return [
            (
                (z >= distance) & (z < LINE - 1),
                self.copy(channel, k, self.c_rows(k, low, 1), self.c_rows(k, low, 1), self.at_up),
                z >= distance + 1,
            ),
            (
                (z <= LINE - 1 - distance) & (z > 0),
                self.copy(channel + 1, k, self.c_rows(k, high, 1), self.c_rows(k, high, 1), self.at_down),
                z <= LINE - 2 - distance,
            ),
        ]

    def sum_hops(self, k):
        z, slot = self.z, lax.rem(k, 4)
        own = self.refs.a_sum.at[slot]
        final = self.refs.a_state.at[lax.rem(k, STATES_A), self.x]
        return {
            A1: [
                (z == 0, self.slotted(A1, k, own, self.at_up)),
                (z == LINE - 1, self.slotted(A1, k, own, self.at_down)),
            ],
            A2: [
                (z == 1, self.slotted(A2, k, own, self.at_up)),
                (z == 2, self.slotted(A2, k, own, self.at_down)),
            ],
            A3: [
                (z == 1, self.copy(A3, k, final, final, self.at_down)),
                (z == 2, self.copy(A3, k, final, final, self.at_up)),
            ],
        }

    def store(self, k):
        r, slot, two = self.refs, lax.rem(k, STATES), lax.rem(k, 2)
        base = k * self.rows
        yield pltpu.make_async_copy(
            r.c_state.at[slot], self.out_ref.at[pl.ds(base, self.rows_c)], r.c_store.at[two]
        )

    def store_a(self, k):
        r, slot, two = self.refs, lax.rem(k, STATES_A), lax.rem(k, 2)
        base = k * self.rows + self.rows_c
        for i in range(2):
            yield pltpu.make_async_copy(
                r.a_state.at[slot, i],
                self.out_ref.at[pl.ds(base + i * self.half, self.half)],
                r.a_store.at[two],
            )

    def step(self, t):
        r, c, h, q = self.refs, self.rows_c, self.half, self.shard
        x, y, z = self.x, self.y, self.z

        def stage(delay, body):
            k = t - delay
            pl.when((k >= 0) & (k < self.rounds))(lambda: body(k))

        def start_if(pairs):
            for condition, copy in pairs:
                pl.when(condition)(copy.start)

        def send_wait_if(pairs):
            for condition, copy in pairs:
                pl.when(condition)(copy.wait_send)

        def begin(k):
            self.core_hop(k).start()
            pl.when(k == 0)(self.load(k).start)

        stage(0, begin)

        def after_core(k):
            two, four = lax.rem(k, 2), lax.rem(k, SLOTS)
            copy = self.core_hop(k)
            copy.wait()
            self.load(k).wait()
            total = lambda i, rows: r.own[i, rows] + r.core_in[four, i, rows]
            everything = pl.ds(0, c)
            r.cy_out[two] = total(1 - y, everything)
            self.cy_hop(k).start()
            for i in range(2):
                rows = pl.ds(pl.multiple_of(c + (1 - x) * h, 16), h)
                r.ax_out[two, i] = total(i, rows)
            self.ax_hop(k).start()
            r.c_state[lax.rem(k, STATES), :] = total(y, everything)
            for i in range(2):
                rows = pl.ds(pl.multiple_of(c + x * h, 16), h)
                r.ax_keep[two, i] = total(i, rows)
            pl.when(k + 1 < self.rounds)(lambda: self.load(k + 1).start())

        stage(1, after_core)

        def second(k):
            two, four, slot = lax.rem(k, 2), lax.rem(k, SLOTS), lax.rem(k, STATES)
            self.cy_hop(k).wait()
            r.c_state[slot] = r.c_state[slot] + r.cy_in[four]
            start_if(self.line_hops(k)[0][1])
            self.ax_hop(k).wait()
            r.ay_out[two] = r.ax_keep[two, 1 - y] + r.ax_in[four, 1 - y]
            self.ay_hop(k).start()
            r.a_sum[lax.rem(k, 4)] = r.ax_keep[two, y] + r.ax_in[four, y]

        stage(2, second)

        def line_step(k, hop):
            name, sends, receives, count = self.line_hops(k)[hop]
            four = lax.rem(k, SLOTS)
            send_wait_if(sends)
            for condition, first in receives:

                @pl.when(condition)
                def _(first=first):
                    sends[0][1].wait_recv()
                    rows = self.c_rows(k, first, count)
                    arrived = (r.ca_in, r.cb_in, r.cc_in)[hop]
                    rows[...] = rows[...] + arrived[four]

            if hop < 2:
                start_if(self.line_hops(k)[hop + 1][1])

        def third(k):
            line_step(k, 0)
            four = lax.rem(k, SLOTS)
            self.ay_hop(k).wait()
            r.a_sum[lax.rem(k, 4)] = r.a_sum[lax.rem(k, 4)] + r.ay_in[four]
            start_if(self.sum_hops(k)[A1])

        stage(3, third)

        def fourth(k):
            line_step(k, 1)
            four, slot = lax.rem(k, SLOTS), lax.rem(k, 4)
            hops = self.sum_hops(k)
            send_wait_if(hops[A1])

            @pl.when((z > 0) & (z < LINE - 1))
            def _():
                hops[A1][0][1].wait_recv()
                r.a_sum[slot] = r.a_sum[slot] + r.a1_in[four]

            start_if(hops[A2])

        stage(4, fourth)

        def fifth(k):
            line_step(k, 2)
            self.cx_hop(k).start()
            four, slot = lax.rem(k, SLOTS), lax.rem(k, 4)
            hops = self.sum_hops(k)
            send_wait_if(hops[A2])

            @pl.when((z > 0) & (z < LINE - 1))
            def _():
                hops[A2][0][1].wait_recv()
                r.a_state[lax.rem(k, STATES_A), x] = r.a_sum[slot] + r.a2_in[four]

            start_if(hops[A3])

        stage(5, fifth)

        def sixth(k):
            four = lax.rem(k, SLOTS)
            hops = self.sum_hops(k)
            send_wait_if(hops[A3])
            pl.when((z == 0) | (z == LINE - 1))(lambda: hops[A3][0][1].wait_recv())
            self.ag_hop(k).start()
            self.cx_hop(k).wait()
            rows = self.c_rows(k, z, 1)
            rows[...] = rows[...] + r.cx_in[four]
            for sends, copy, _ in self.gather_hops(k, 0):
                pl.when(sends)(copy.start)

        stage(6, sixth)

        def gather_step(k, distance):
            for sends, copy, receives in self.gather_hops(k, distance):
                pl.when(sends)(copy.wait_send)
                pl.when(receives)(copy.wait_recv)
            if distance < 2:
                for sends, copy, _ in self.gather_hops(k, distance + 1):
                    pl.when(sends)(copy.start)

        def seventh(k):
            gather_step(k, 0)
            self.ag_hop(k).wait()
            for copy in self.store_a(k):
                copy.start()

        stage(7, seventh)

        def eighth(k):
            gather_step(k, 1)
            for copy in self.store_a(k):
                copy.wait()

        stage(8, eighth)

        def ninth(k):
            gather_step(k, 2)
            for copy in self.store(k):
                copy.start()

        stage(9, ninth)

        def tenth(k):
            for copy in self.store(k):
                copy.wait()

        stage(10, tenth)

    def cy_hop(self, k):
        return self.slotted(CY, k, self.refs.cy_out.at[lax.rem(k, 2)], self.at_y)

    def ax_hop(self, k):
        return self.slotted(AX, k, self.refs.ax_out.at[lax.rem(k, 2)], self.at_x)

    def ay_hop(self, k):
        return self.slotted(AY, k, self.refs.ay_out.at[lax.rem(k, 2)], self.at_y)

    def cx_hop(self, k):
        return self.slotted(CX, k, self.c_rows(k, self.z, 1), self.at_x)

    def ag_hop(self, k):
        final = self.refs.a_state.at[lax.rem(k, STATES_A), self.x]
        return self.copy(AG, k, final, final, self.at_x)


class VectorSum:
    def __init__(self, reducer, value, arrived, send, recv):
        self.value, self.arrived, self.send, self.recv = value, arrived, send, recv
        self.net = reducer

    def hop(self, index, device):
        return pltpu.make_async_remote_copy(
            src_ref=self.value,
            dst_ref=self.arrived.at[index],
            send_sem=self.send.at[index],
            recv_sem=self.recv.at[index],
            device_id=device,
            device_id_type=MESH,
        )

    def exchange(self, index):
        return self.hop(index, (self.net.at_core, self.net.at_y, self.net.at_x)[index])

    def step(self, at):
        z, value, arrived = self.net.z, self.value, self.arrived
        middle = (z > 0) & (z < LINE - 1)
        sends = {
            3: ((z == 0, self.net.at_up), (z == LINE - 1, self.net.at_down)),
            4: ((z == 1, self.net.at_up), (z == 2, self.net.at_down)),
            5: ((z == 1, self.net.at_down), (z == 2, self.net.at_up)),
        }

        def start(index):
            for condition, device in sends[index]:
                pl.when(condition)(self.hop(index, device).start)

        def finish(index, receives, add):
            for condition, device in sends[index]:
                pl.when(condition)(self.hop(index, device).wait_send)

            @pl.when(receives)
            def _():
                self.hop(index, sends[index][0][1]).wait_recv()
                value[...] = arrived[index] + value[...] if add else arrived[index]

        def first():
            self.exchange(0).start()

        def pair(index):
            self.exchange(index).wait()
            value[...] = value[...] + arrived[index]
            if index < 2:
                self.exchange(index + 1).start()
            else:
                start(3)

        def outer():
            finish(3, middle, True)
            start(4)

        def inner():
            finish(4, middle, True)
            start(5)

        pl.when(at == 0)(first)
        for index in range(3):
            pl.when(at == index + 1)(functools.partial(pair, index))
        pl.when(at == 4)(outer)
        pl.when(at == 5)(inner)
        pl.when(at == 6)(lambda: finish(5, (z == 0) | (z == LINE - 1), False))


LANES = 128
PARTS = 4
WIDE = 1152


def gelu_both(u):
    c0, c1 = 0.7978845608028654, 0.044715
    square = u * u
    t = jnp.tanh(c0 * u * (1.0 + c1 * square))
    half = 0.5 + 0.5 * t
    slope = half + (0.5 * c0) * u * (1.0 - t * t) * (1.0 + (3.0 * c1) * square)
    return u * half, slope


def norm_rows(values):
    centred = values - jnp.mean(values, axis=-1, keepdims=True)
    inverse = lax.rsqrt(jnp.mean(centred * centred, axis=-1, keepdims=True) + 1e-05)
    return centred * inverse, inverse


def norm_rows_back(grad_hat, normed, inverse):
    mean_grad = jnp.mean(grad_hat, axis=-1, keepdims=True)
    mean_cross = jnp.mean(grad_hat * normed, axis=-1, keepdims=True)
    return inverse * (grad_hat - mean_grad - normed * mean_cross)


def column_sum(values):
    return jnp.sum(values, axis=0, keepdims=True)


def block(i, count):
    return pl.ds(pl.multiple_of(i * count, count), count)


def identity(size):
    row = lax.broadcasted_iota(jnp.int32, (size, size), 0)
    column = lax.broadcasted_iota(jnp.int32, (size, size), 1)
    return jnp.where(row == column, 1.0, 0.0).astype(BF16)


def turned(eye, rows):
    width = rows.shape[1]
    pieces = []
    for at in range(0, width, LANES):
        size = min(LANES, width - at)
        pieces.append(dot(eye[:size, :size], rows[:, at : at + size], NT))
    return jnp.concatenate(pieces, axis=0)


def leftover_rows(tiles):
    first, second, third = tiles
    return [
        [first[:96]],
        [second[:64], first[96:]],
        [third[:32], second[64:]],
        [third[32:]],
    ]


def layer_kernel(reducer, names, *refs):
    r = types.SimpleNamespace(**dict(zip(names, refs)))
    width, part_rows = r.tokens.shape[1:]
    seq = PARTS * part_rows
    feat, ff = width // PARTS, r.w_up.shape[1] // PARTS
    main = ff // LANES
    left = ff - main * LANES
    stride = (r.w_up.shape[1] // LANES - main) // (PARTS - 1)
    heads, group = width // HD, 5
    reducer.bind(r.parts, r.total, r)
    narrow, y = reducer.narrow, reducer.y
    gain1, bias1, gain2, bias2, bias_down = (
        ref[...].reshape(1, width) for ref in (r.gain1, r.bias1, r.gain2, r.bias2, r.bias_down)
    )
    eye = identity(LANES)
    vec = r.vec
    vector_sum = VectorSum(reducer, vec, r.vec_in, r.vec_send, r.vec_recv)

    def local(index, source, target):
        return pltpu.make_async_copy(source, target, r.local.at[index])

    def spread(j, source, target):
        remote = [
            pltpu.make_async_remote_copy(
                src_ref=source.at[device[1]],
                dst_ref=target.at[narrow],
                send_sem=r.spread_send.at[j, d],
                recv_sem=r.spread_recv.at[j, d],
                device_id=device,
                device_id_type=MESH,
            )
            for d, device in enumerate((reducer.at_core, reducer.at_y, reducer.at_cross))
        ]
        return remote, local(j, source.at[narrow], target.at[narrow])

    def weights(i, tiles):
        two = lax.rem(i, 2)
        return [
            pltpu.make_async_copy(
                source.at[:, pl.ds(pl.multiple_of(tile * LANES, LANES), LANES)],
                target.at[two, :, pl.ds(q * LANES, LANES)],
                r.w_load.at[two, n, q],
            )
            for n, (source, target) in enumerate(((r.w_up, r.w_up_in), (r.w_down, r.w_down_in)))
            for q, tile in enumerate(tiles)
        ]

    main_tiles = lambda i: [i + stride * q for q in range(PARTS)]
    left_tiles = [main + stride * q for q in range(PARTS - 1)]

    squares = [local(4 + j, r.w_qkv.at[j], r.square.at[j]) for j in range(3)]
    for copy in squares:
        copy.start()
    reducer.barrier()
    tokens, tokens_own = spread(0, r.tokens, r.x_in)
    cots, cots_own = spread(1, r.cot, r.c_in)
    for copy in tokens + [tokens_own]:
        copy.start()
    for copy in weights(0, main_tiles(0)):
        copy.start()
    vec[...] = jnp.zeros_like(vec)
    for target in (r.q, r.k, r.v, r.m, r.g):
        target[:, width:] = jnp.zeros((seq, WIDE - width), BF16)
    r.acc[...] = jnp.zeros_like(r.acc)
    row = lax.broadcasted_iota(jnp.int32, (seq, seq), 0)
    column = lax.broadcasted_iota(jnp.int32, (seq, seq), 1)
    length = r.lengths[narrow]
    r.bias[...] = jnp.where((column <= row) & (column < length), 0.0, -1e30)
    r.up_bias[...] = r.bias_up[...].reshape(r.up_bias.shape)

    def first_norm(i):
        rows = block(i, part_rows)
        x = dot(eye, r.x_in[i], NT)
        r.x[rows] = x.astype(BF16)
        normed, _ = norm_rows(x)
        r.h[rows] = (normed * gain1 + bias1).astype(BF16)

    def project(side):
        rows = block(side, seq // 2)
        for j, target in enumerate((r.q, r.k, r.v)):
            target[rows, :width] = dot(r.h[rows], r.square[j], NN).astype(BF16)

    tokens_own.wait()
    first_norm(narrow)
    tokens[0].wait()
    first_norm(tokens_peer(reducer, 0))
    for copy in squares:
        copy.wait()
    project(y)
    for d in (1, 2):
        tokens[d].wait()
        first_norm(tokens_peer(reducer, d))
    for copy in cots + [cots_own]:
        copy.start()
    project(1 - y)
    w_out = local(4, r.w_out, r.square.at[0])
    w_out.start()

    def head_at(h):
        return pl.multiple_of(jnp.minimum(h * HD // LANES * LANES, WIDE - 256), LANES)

    def forward(i, carry):
        pair = [(h, head_at(h)) for h in (2 * i, 2 * i + 1)]
        attend_heads(pair, r.q, r.k, r.v, r.m, r.bias)
        return carry

    lax.fori_loop(0, heads // 2, forward, 0)
    w_out.wait()

    def second_norm(i, carry):
        rows = block(i, part_rows)
        after = r.x[rows].astype(F32) + dot(r.m[rows, :width], r.square[0], NN)
        r.rows[rows] = after
        normed, _ = norm_rows(after)
        r.h[rows] = (normed * gain2 + bias2).astype(BF16)
        return carry

    lax.fori_loop(0, PARTS, second_norm, 0)
    for copy in cots + [cots_own]:
        copy.wait()
    for i in range(PARTS):
        r.grad[block(i, part_rows)] = dot(eye, r.c_in[i], NT).astype(BF16)

    upper = pl.ds(0, seq)
    lower = pl.ds(seq, seq)

    def put(count, base):
        return [
            local(
                8 + q,
                r.stage.at[pl.ds(2 * LANES * q, count)],
                r.parts.at[q // 2, q % 2, pl.ds(base, count)],
            )
            for q in range(PARTS)
        ]

    def put_block(i):
        return put(2 * LANES, pl.multiple_of(i * 2 * LANES, 2 * LANES))

    def feed_forward(i, tiles):
        two, count = lax.rem(i, 2), LANES * len(tiles)
        up, down = r.w_up_in[two, :, :count], r.w_down_in[two, :, :count]
        at = [pl.ds(pl.multiple_of(tile * LANES, LANES), LANES) for tile in tiles]
        bias = jnp.concatenate([r.up_bias[:, lanes] for lanes in at], axis=1)
        hidden, cot = r.h[...], r.grad[...]
        act, slope = gelu_both(dot(hidden, up, NN) + bias)
        act = act.astype(BF16)
        grad_up = (dot(cot, down, NN) * slope).astype(BF16)
        r.acc[upper, :width] += dot(act, down, NT)
        r.acc[lower, :width] += dot(grad_up, up, NT)
        total = column_sum(grad_up.astype(F32))
        for q, lanes in enumerate(at):
            vec[0:1, lanes] = total[:, LANES * q : LANES * (q + 1)]
        return dot(act, cot, TN).astype(BF16), dot(grad_up, hidden, TN).astype(BF16)

    def ff_block(i, carry):
        for copy in weights(i, main_tiles(i)):
            copy.wait()

        @pl.when(i + 1 < main)
        def _():
            for copy in weights(i + 1, main_tiles(i + 1)):
                copy.start()

        @pl.when(i + 1 == main)
        def _():
            for copy in weights(main, left_tiles):
                copy.start()

        values = feed_forward(i, main_tiles(i))

        @pl.when(i > 1)
        def _():
            for copy in put_block(i - 1):
                copy.wait()

        for j, value in enumerate(values):
            for q in range(PARTS):
                r.stage[LANES * (2 * q + j) : LANES * (2 * q + j + 1)] = value[
                    LANES * q : LANES * (q + 1)
                ]
        for copy in put_block(i):
            copy.start()
        return carry

    ff_block(0, 0)
    for copy in put_block(0):
        copy.wait()
    reducer.step(jnp.int32(0))

    def ff_step(s, carry):
        lax.fori_loop(2 * s - 1, 2 * s + 1, ff_block, 0)
        reducer.step(s)
        return carry

    ff_steps = main // 2
    lax.fori_loop(1, ff_steps, ff_step, 0)
    lax.fori_loop(main - 1, main, ff_block, 0)
    for copy in weights(main, left_tiles):
        copy.wait()
    values = feed_forward(main, left_tiles)
    for copy in put_block(main - 1):
        copy.wait()
    for j, value in enumerate(values):
        tiles = [value[LANES * q : LANES * (q + 1)] for q in range(PARTS - 1)]
        for q, pieces in enumerate(leftover_rows(tiles)):
            at = 2 * LANES * q + left * j
            for piece in pieces:
                r.stage[at : at + piece.shape[0]] = piece
                at += piece.shape[0]
    put_left = put(2 * left, 2 * LANES * main)
    for copy in put_left:
        copy.start()
    reducer.step(jnp.int32(ff_steps))
    done = ff_steps + 1
    for copy in put_left:
        copy.wait()

    def add_vector(index, value):
        vec[index : index + 1, :width] = vec[index : index + 1, :width] + value

    def middle_rows(i, carry):
        rows = block(i, part_rows)
        after = r.rows[rows]
        result = r.acc[rows, :width] + after + bias_down
        r.x_in[i] = turned(eye, result.astype(BF16)).astype(BF16)
        normed, inverse = norm_rows(after)
        grad = r.acc[pl.ds(pl.multiple_of(seq + i * part_rows, part_rows), part_rows), :width]
        cot = r.grad[rows].astype(F32)
        add_vector(3, column_sum(grad * normed))
        add_vector(4, column_sum(grad))
        add_vector(5, column_sum(cot))
        grad_after = cot + norm_rows_back(grad * gain2, normed, inverse)
        r.rows[rows] = grad_after
        r.grad[rows] = grad_after.astype(BF16)
        return carry

    lax.fori_loop(0, PARTS, middle_rows, 0)
    r.g[:, :width] = dot(r.grad[...], r.square[0], NT).astype(BF16)
    w_query = local(4, r.w_qkv.at[0], r.square.at[0])
    w_query.start()

    def head_step(s, carry):
        def one(h, carry):
            head_back(h, head_at(h), r.q, r.k, r.v, r.g, r.bias)
            return carry

        lax.fori_loop(s * group, (s + 1) * group, one, 0)
        reducer.step(done + s)
        return carry

    lax.fori_loop(0, heads // group, head_step, 0)
    done += heads // group

    def first_again(i, carry):
        rows = block(i, part_rows)
        normed, _ = norm_rows(r.x[rows].astype(F32))
        r.h[rows] = (normed * gain1 + bias1).astype(BF16)
        return carry

    lax.fori_loop(0, PARTS, first_again, 0)
    lefts = [(r.m, r.grad), (r.q, r.h), (r.k, r.h), (r.v, r.h)]
    size = 2 * feat

    def tail_put(turn):
        pair, quarter = turn // PARTS, turn % PARTS
        return local(
            8 + turn % 2,
            r.stage.at[pl.ds(size * (turn % 2), size)],
            r.parts.at[quarter // 2, quarter % 2, pl.ds(2 * ff + size * pair, size)],
        )

    for turn in range(2 * PARTS):
        pair, quarter = turn // PARTS, turn % PARTS
        start = feat * quarter // LANES * LANES
        offset = feat * quarter - start
        products = [
            dot(one[:, start : start + 384], two[...], TN)
            for one, two in lefts[2 * pair : 2 * pair + 2]
        ]
        if turn >= 2 and turn % PARTS >= 2:
            tail_put(turn - 2).wait()
        for p in range(5):
            units = [
                products[u // 5][offset + u % 5 * HD : offset + u % 5 * HD + HD]
                for u in (2 * p, 2 * p + 1)
            ]
            at = size * (turn % 2) + 2 * HD * p
            r.stage[at : at + 2 * HD] = jnp.concatenate(units, axis=0).astype(BF16)
        tail_put(turn).start()
        if turn % PARTS == PARTS - 1:
            tail_put(turn - 1).wait()
            tail_put(turn).wait()
            reducer.step(jnp.int32(done))
            done += 1
    w_query.wait()
    r.acc[upper, :width] = dot(r.q[:, :width], r.square[0], NT)
    r.acc[upper, :width] += dot(r.k[:, :width], r.square[1], NT)
    reducer.step(jnp.int32(done))
    done += 1
    r.acc[upper, :width] += dot(r.v[:, :width], r.square[2], NT)

    def last_norm(i, carry):
        rows = block(i, part_rows)
        normed, inverse = norm_rows(r.x[rows].astype(F32))
        grad = r.acc[rows, :width]
        add_vector(1, column_sum(grad * normed))
        add_vector(2, column_sum(grad))
        back = r.rows[rows] + norm_rows_back(grad * gain1, normed, inverse)
        r.c_in[i] = turned(eye, back.astype(BF16)).astype(BF16)
        return carry

    lax.fori_loop(0, PARTS, last_norm, 0)

    steps = reducer.rounds + 11
    outs, outs_own = spread(2, r.x_in, r.output)
    grads, grads_own = spread(3, r.c_in, r.input_grad)
    turn = 32 * narrow
    lane = lax.broadcasted_iota(jnp.int32, (1, LANES), 1)

    def mix(tile, mask, value):
        lanes = pl.ds(pl.multiple_of(tile * LANES, LANES), LANES)
        r.acc[:, lanes] = jnp.where(mask, value, r.acc[:, lanes])

    def settle(j):
        base = pl.multiple_of(j * 2 * LANES, 2 * LANES)
        place = pl.multiple_of(turn + j * LANES, 32)
        get = local(4, r.total.at[pl.ds(base, 2 * LANES)], r.stage.at[pl.ds(0, 2 * LANES)])
        get.start()
        get.wait()
        give = local(5, r.stage.at[pl.ds(0, LANES)], r.down.at[pl.ds(place, LANES)])
        give.start()
        value = pltpu.roll(turned(eye, r.stage[LANES : 2 * LANES]), turn, 1)
        mix(j, lane >= turn, value)
        mix(j + 1, lane < turn, value)
        give.wait()

    def settle_left():
        get = local(4, r.total.at[pl.ds(2 * LANES * main, 2 * left)], r.stage.at[pl.ds(0, 2 * left)])
        get.start()
        get.wait()
        gives = []
        for piece in range(left // 32):
            place = lax.rem(turn + main * LANES + 32 * piece, ff)
            gives.append(
                local(
                    8 + piece,
                    r.stage.at[pl.ds(32 * piece, 32)],
                    r.down.at[pl.ds(pl.multiple_of(place, 32), 32)],
                )
            )
            gives[-1].start()
        value = turned(eye, r.stage[left : left + LANES])
        mix(main, (lane >= turn) & (lane < left), pltpu.roll(value, turn, 1))
        mix(0, lane < turn, pltpu.roll(value, lax.rem(turn + LANES - left, LANES), 1))
        r.square[0] = r.acc[:, :ff].astype(BF16)
        local(6, r.square.at[0], r.up).start()
        for copy in gives:
            copy.wait()

    def drain(t, carry):
        reducer.step(t)

        @pl.when(t == reducer.rounds + 1)
        def _():
            for copy in outs + [outs_own] + grads + [grads_own]:
                copy.start()

        vector_sum.step(t - reducer.rounds)
        at = t - done
        pl.when(at < main)(lambda: settle(at))
        pl.when(at == main)(settle_left)
        return carry

    lax.fori_loop(done, steps, drain, 0)
    finish = local(7, vec, r.vector)
    finish.start()
    for copy in outs + [outs_own] + grads + [grads_own]:
        copy.wait()
    local(6, r.square.at[0], r.up).wait()
    finish.wait()


def tokens_peer(reducer, d):
    return (reducer.at_core, reducer.at_y, reducer.at_cross)[d][1]


def softmax_parts(scores):
    expo = jnp.exp(scores - jnp.max(scores, axis=1, keepdims=True))
    return expo * (1.0 / jnp.sum(expo, axis=1, keepdims=True))


def attend_heads(pair, q_ref, k_ref, v_ref, out_ref, bias_ref):
    half = q_ref.shape[0] // 2
    results = []
    for h, start in pair:
        window = pl.ds(start, 256)
        mask = head_mask(h, start, 256)
        query = jnp.where(mask, q_ref[:, window], 0)
        keys, values = k_ref[:, window], v_ref[:, window]
        for part in range(2):
            count = (part + 1) * half
            rows = slice(part * half, count)
            scores = dot(query[rows], keys[:count], NT) * SCALE + bias_ref[rows, :count]
            probs = softmax_parts(scores).astype(BF16)
            mixed = dot(probs, values[:count], NN).astype(BF16)
            results.append((rows, window, mask, mixed))
    for rows, window, mask, mixed in results:
        out_ref[rows, window] = jnp.where(mask, mixed, out_ref[rows, window])


def head_back(h, start, q_ref, k_ref, v_ref, grad_ref, bias_ref):
    half = q_ref.shape[0] // 2
    window = pl.ds(start, 256)
    mask = head_mask(h, start, 256)
    query = jnp.where(mask, q_ref[:, window], 0)
    grad = jnp.where(mask, grad_ref[:, window], 0)
    keys, values = k_ref[:, window], v_ref[:, window]
    grads = []
    for part in range(2):
        count = (part + 1) * half
        rows = slice(part * half, count)
        scores = dot(query[rows], keys[:count], NT) * SCALE + bias_ref[rows, :count]
        grad_probs = dot(grad[rows], values[:count], NT)
        probs = softmax_parts(scores)
        inner = jnp.sum(probs * grad_probs, axis=1, keepdims=True)
        grad_scores = (probs * (grad_probs - inner) * SCALE).astype(BF16)
        gq = dot(grad_scores, keys[:count], NN).astype(BF16)
        gk = dot(grad_scores, query[rows], TN)
        gv = dot(probs.astype(BF16), grad[rows], TN)
        grads.append((gq, gk, gv))
    (gq0, gk0, gv0), (gq1, gk1, gv1) = grads
    q_ref[:half, window] = jnp.where(mask, gq0, q_ref[:half, window])
    q_ref[half:, window] = jnp.where(mask, gq1, q_ref[half:, window])
    for ref, first, second in ((k_ref, gk0, gk1), (v_ref, gv0, gv1)):
        top, bottom = (first + second[:half]).astype(BF16), second[half:].astype(BF16)
        ref[:half, window] = jnp.where(mask, top, ref[:half, window])
        ref[half:, window] = jnp.where(mask, bottom, ref[half:, window])


def whole_layer(**arrays):
    parts, width, part_rows = arrays["tokens"].shape
    seq, hidden = parts * part_rows, arrays["w_up"].shape[1]
    ff = hidden // parts
    rows = 2 * ff + width
    reducer = Reducer(128, 96, width)
    scratch = reducer.scratch()
    low = lambda *shape: pltpu.VMEM(shape, BF16)
    full = lambda *shape: pltpu.VMEM(shape, F32)
    dma = lambda *shape: pltpu.SemaphoreType.DMA(shape)
    scratch.update(
        x_in=low(parts, width, part_rows),
        c_in=low(parts, width, part_rows),
        w_up_in=low(2, width, parts * LANES),
        w_down_in=low(2, width, parts * LANES),
        stage=low(width, width),
        square=low(3, width, width),
        q=low(seq, WIDE),
        k=low(seq, WIDE),
        v=low(seq, WIDE),
        m=low(seq, WIDE),
        g=low(seq, WIDE),
        h=low(seq, width),
        grad=low(seq, width),
        x=low(seq, width),
        rows=full(seq, width),
        acc=full(width, WIDE),
        bias=full(seq, seq),
        up_bias=full(1, hidden),
        vec=full(8, hidden),
        vec_in=full(6, 8, hidden),
        vec_send=dma(6),
        vec_recv=dma(6),
        local=dma(12),
        w_load=dma(2, 2, parts),
        spread_send=dma(4, 3),
        spread_recv=dma(4, 3),
    )
    hbm = pl.BlockSpec(memory_space=pl.ANY)
    vmem = pl.BlockSpec(memory_space=pltpu.VMEM)
    low_out = lambda *shape: jax.ShapeDtypeStruct(shape, BF16)
    outputs = dict(
        parts=low_out(2, parts // 2, rows, width),
        total=low_out(rows, width),
        down=low_out(ff, width),
        up=low_out(width, ff),
        output=low_out(parts, width, part_rows),
        input_grad=low_out(parts, width, part_rows),
        vector=jax.ShapeDtypeStruct((8, hidden), F32),
    )
    smem = pl.BlockSpec(memory_space=pltpu.SMEM)
    names = list(arrays) + list(outputs) + list(scratch)
    results = pl.pallas_call(
        functools.partial(layer_kernel, reducer, names),
        out_shape=tuple(outputs.values()),
        in_specs=[hbm] * 6 + [smem] + [vmem] * (len(arrays) - 7),
        out_specs=[hbm] * len(outputs),
        scratch_shapes=list(scratch.values()),
        compiler_params=pltpu.CompilerParams(
            collective_id=0, has_side_effects=True, vmem_limit_bytes=VMEM_LIMIT
        ),
        name="whole_layer",
    )(*arrays.values())
    return types.SimpleNamespace(**dict(zip(outputs, results)))


def on_device(
    wide,
    tokens,
    lengths,
    norm1_gain,
    norm1_bias,
    w_qkv,
    w_out,
    norm2_gain,
    norm2_bias,
    w_up,
    bias_up,
    w_down,
    bias_down,
    cotangent,
):
    narrow = lax.axis_index("narrow")
    width, hidden = w_up.shape
    parts = tokens.shape[0]
    ff, feat = hidden // parts, width // parts
    got = whole_layer(
        tokens=tokens.transpose(0, 2, 1),
        cot=cotangent.transpose(0, 2, 1),
        w_qkv=w_qkv.transpose(1, 0, 2),
        w_out=w_out,
        w_up=w_up,
        w_down=w_down.T,
        lengths=lengths,
        gain1=norm1_gain,
        bias1=norm1_bias,
        gain2=norm2_gain,
        bias2=norm2_bias,
        bias_up=bias_up,
        bias_down=bias_down,
    )
    rest, down, up, vector = got.total[2 * ff :], got.down, got.up, got.vector
    if wide > BLOCK:
        groups = [list(range(i, wide, BLOCK)) for i in range(BLOCK)]
        rest, down, up, vector = (
            lax.psum(a.astype(F32), "wide", axis_index_groups=groups)
            for a in (rest, down, up, vector)
        )
    qkv = rest[feat:].astype(F32).reshape(3, feat, width).transpose(2, 0, 1)
    mine = lambda v: lax.dynamic_slice_in_dim(v, narrow * (v.shape[0] // parts), v.shape[0] // parts)
    up_bias = mine(vector[0])
    gain1, bias1, gain2, bias2, down_bias = (mine(vector[i, :width]) for i in range(1, 6))
    return (
        got.output.transpose(0, 2, 1),
        got.input_grad.transpose(0, 2, 1).astype(F32),
        gain1,
        bias1,
        qkv,
        rest[:feat].astype(F32),
        gain2,
        bias2,
        up.astype(F32),
        up_bias,
        down.astype(F32),
        down_bias,
    )


def solution(mesh):
    rows = P("wide", "narrow", None)
    in_specs = (rows, P("wide")) + (P(),) * 10 + (rows,)
    out_specs = (
        rows,
        rows,
        P("narrow"),
        P("narrow"),
        P(None, None, "narrow"),
        P("narrow", None),
        P("narrow"),
        P("narrow"),
        P(None, "narrow"),
        P("narrow"),
        P("narrow", None),
        P("narrow"),
    )
    return jax.shard_map(
        functools.partial(on_device, mesh.shape["wide"]),
        mesh=mesh,
        in_specs=in_specs,
        out_specs=out_specs,
        check_vma=False,
    )
```

```python
import functools
import types

import jax
import jax.numpy as jnp
from jax import lax
from jax.experimental import pallas as pl
from jax.experimental.pallas import tpu as pltpu
from jax.sharding import PartitionSpec as P

HD = 56
SCALE = HD**-0.5
F32, BF16 = jnp.float32, jnp.bfloat16
MESH = pl.DeviceIdType.MESH
VMEM_LIMIT = 62 * 1024 * 1024
LINE, PAIR = 4, 2
BLOCK = LINE * PAIR
SLOTS = 4
CORE, CY, CA, CB, CC, CX, AX, AY, A1, A2, A3, AG, GATHER = range(13)
CHANNELS = GATHER + 6


def dot(a, b, dims):
    return lax.dot_general(a, b, (dims, ((), ())), preferred_element_type=F32)


NN, NT, TN = ((1,), (0,)), ((1,), (1,)), ((0,), (0,))


def head_mask(h, start, size):
    lane = start + lax.broadcasted_iota(jnp.int32, (1, size), 1)
    return (lane >= h * HD) & (lane < h * HD + HD)


class Reducer:
    hops = 9

    def __init__(self, rows_c, rows_a, width, total):
        self.rounds = total // (rows_c + rows_a)
        self.states, self.states_a = 10, 8
        self.rows_c, self.rows_a, self.width = rows_c, rows_a, width
        self.rows = rows_c + rows_a
        self.shard, self.half = rows_c // LINE, rows_a // 2

    def scratch(self):
        c, a, q, h, d = self.rows_c, self.rows_a, self.shard, self.half, self.width
        buffers = dict(
            own=(2, self.rows, d),
            core_in=(2, 2, self.rows, d),
            cy_out=(2, c, d),
            cy_in=(SLOTS, c, d),
            c_state=(self.states, c, d),
            ca_in=(SLOTS, 3 * q, d),
            cb_in=(SLOTS, 2 * q, d),
            cc_in=(SLOTS, q, d),
            cx_in=(SLOTS, q, d),
            ax_out=(2, 2, h, d),
            ax_keep=(2, 2, h, d),
            ax_in=(SLOTS, 2, h, d),
            ay_out=(2, h, d),
            ay_in=(SLOTS, h, d),
            a_sum=(4, h, d),
            a1_in=(SLOTS, h, d),
            a2_in=(SLOTS, h, d),
            a_state=(self.states_a, 2, h, d),
        )
        result = {name: pltpu.VMEM(shape, BF16) for name, shape in buffers.items()}
        result.update(
            net_send=pltpu.SemaphoreType.DMA((CHANNELS, SLOTS)),
            net_recv=pltpu.SemaphoreType.DMA((CHANNELS, SLOTS)),
            load=pltpu.SemaphoreType.DMA((2,)),
            c_store=pltpu.SemaphoreType.DMA((2,)),
            a_store=pltpu.SemaphoreType.DMA((2,)),
        )
        return result

    def bind(self, part_ref, out_ref, refs):
        self.part_ref, self.out_ref, self.refs = part_ref, out_ref, refs
        wide, narrow = lax.axis_index("wide"), lax.axis_index("narrow")
        self.wide, self.narrow = wide, narrow
        self.z, self.x = lax.rem(wide, BLOCK) // PAIR, lax.rem(wide, PAIR)
        self.y, self.core = narrow // 2, lax.rem(narrow, 2)
        flip = lambda index, bit: index + 1 - 2 * bit
        self.at_core = (wide, flip(narrow, self.core))
        self.at_y = (wide, narrow + 2 - 4 * self.y)
        self.at_cross = (wide, flip(narrow, self.core) + 2 - 4 * self.y)
        self.at_x = (flip(wide, self.x), narrow)
        self.at_up = (wide + PAIR, narrow)
        self.at_down = (wide - PAIR, narrow)

    def barrier(self):
        z = self.z
        barrier = pltpu.get_barrier_semaphore()

        def greet(target):
            pl.semaphore_signal(barrier, inc=1, device_id=target, device_id_type=MESH)

        for target in (self.at_core, self.at_y, self.at_cross, self.at_x):
            greet(target)
        pl.when(z < LINE - 1)(lambda: greet(self.at_up))
        pl.when(z > 0)(lambda: greet(self.at_down))
        edge = (z == 0) | (z == LINE - 1)
        pl.when(edge)(lambda: pl.semaphore_wait(barrier, 5))
        pl.when(~edge)(lambda: pl.semaphore_wait(barrier, 6))

    def copy(self, channel, k, source, target, device):
        slot = lax.rem(k, SLOTS)
        return pltpu.make_async_remote_copy(
            src_ref=source,
            dst_ref=target,
            send_sem=self.refs.net_send.at[channel, slot],
            recv_sem=self.refs.net_recv.at[channel, slot],
            device_id=device,
            device_id_type=MESH,
        )


    def load(self, k):
        r = self.refs
        return pltpu.make_async_copy(
            self.part_ref.at[:, self.core, pl.ds(k * self.rows, self.rows)],
            r.own,
            r.load.at[lax.rem(k, 2)],
        )

    def core_hop(self, k):
        return self.copy(
            CORE,
            k,
            self.part_ref.at[:, 1 - self.core, pl.ds(k * self.rows, self.rows)],
            self.refs.core_in.at[lax.rem(k, 2)],
            self.at_core,
        )

    def slotted(self, channel, k, source, device):
        r = self.refs
        arrivals = {CY: r.cy_in, CA: r.ca_in, CB: r.cb_in, CC: r.cc_in, CX: r.cx_in}
        arrivals.update({AX: r.ax_in, AY: r.ay_in, A1: r.a1_in, A2: r.a2_in})
        return self.copy(channel, k, source, arrivals[channel].at[lax.rem(k, SLOTS)], device)

    def c_rows(self, k, first, count):
        return self.refs.c_state.at[
            lax.rem(k, self.states), pl.ds(pl.multiple_of(first * self.shard, self.shard), count * self.shard)
        ]

    def line_hops(self, k):
        z, up, down = self.z, self.at_up, self.at_down
        hops = []
        for name, count, up_from in ((CA, 3, 0), (CB, 2, 1), (CC, 1, 2)):
            down_from = LINE - 1 - up_from
            hops.append(
                (
                    name,
                    [
                        (z == up_from, self.slotted(name, k, self.c_rows(k, LINE - count, count), up)),
                        (z == down_from, self.slotted(name, k, self.c_rows(k, 0, count), down)),
                    ],
                    [(z == up_from + 1, LINE - count), (z == down_from - 1, 0)],
                    count,
                )
            )
        return hops

    def gather_hops(self, k, distance):
        z = self.z
        channel = GATHER + 2 * distance
        low, high = jnp.maximum(z - distance, 0), jnp.minimum(z + distance, LINE - 1)
        return [
            (
                (z >= distance) & (z < LINE - 1),
                self.copy(channel, k, self.c_rows(k, low, 1), self.c_rows(k, low, 1), self.at_up),
                z >= distance + 1,
            ),
            (
                (z <= LINE - 1 - distance) & (z > 0),
                self.copy(channel + 1, k, self.c_rows(k, high, 1), self.c_rows(k, high, 1), self.at_down),
                z <= LINE - 2 - distance,
            ),
        ]

    def sum_hops(self, k):
        z, slot = self.z, lax.rem(k, 4)
        own = self.refs.a_sum.at[slot]
        final = self.refs.a_state.at[lax.rem(k, self.states_a), self.x]
        return {
            A1: [
                (z == 0, self.slotted(A1, k, own, self.at_up)),
                (z == LINE - 1, self.slotted(A1, k, own, self.at_down)),
            ],
            A2: [
                (z == 1, self.slotted(A2, k, own, self.at_up)),
                (z == 2, self.slotted(A2, k, own, self.at_down)),
            ],
            A3: [
                (z == 1, self.copy(A3, k, final, final, self.at_down)),
                (z == 2, self.copy(A3, k, final, final, self.at_up)),
            ],
        }

    def store(self, k):
        r, slot, two = self.refs, lax.rem(k, self.states), lax.rem(k, 2)
        base = k * self.rows
        yield pltpu.make_async_copy(
            r.c_state.at[slot], self.out_ref.at[pl.ds(base, self.rows_c)], r.c_store.at[two]
        )

    def store_a(self, k):
        r, slot, two = self.refs, lax.rem(k, self.states_a), lax.rem(k, 2)
        base = k * self.rows + self.rows_c
        for i in range(2):
            yield pltpu.make_async_copy(
                r.a_state.at[slot, i],
                self.out_ref.at[pl.ds(base + i * self.half, self.half)],
                r.a_store.at[two],
            )

    def step(self, t):
        r, c, h, q = self.refs, self.rows_c, self.half, self.shard
        x, y, z = self.x, self.y, self.z

        def stage(delay, body):
            k = t - delay
            pl.when((k >= 0) & (k < self.rounds))(lambda: body(k))

        def start_if(pairs):
            for condition, copy in pairs:
                pl.when(condition)(copy.start)

        def send_wait_if(pairs):
            for condition, copy in pairs:
                pl.when(condition)(copy.wait_send)

        def begin(k):
            self.core_hop(k).start()
            pl.when(k == 0)(self.load(k).start)


        def after_core(k):
            two, four = lax.rem(k, 2), lax.rem(k, SLOTS)
            copy = self.core_hop(k)
            copy.wait()
            self.load(k).wait()
            total = lambda i, rows: r.own[i, rows] + r.core_in[two, i, rows]
            everything = pl.ds(0, c)
            r.cy_out[two] = total(1 - y, everything)
            self.cy_hop(k).start()
            for i in range(2):
                rows = pl.ds(pl.multiple_of(c + (1 - x) * h, 16), h)
                r.ax_out[two, i] = total(i, rows)
            self.ax_hop(k).start()
            r.c_state[lax.rem(k, self.states), :] = total(y, everything)
            for i in range(2):
                rows = pl.ds(pl.multiple_of(c + x * h, 16), h)
                r.ax_keep[two, i] = total(i, rows)
            pl.when(k + 1 < self.rounds)(lambda: self.load(k + 1).start())

        stage(1, after_core)
        stage(0, begin)

        def second(k):
            two, four, slot = lax.rem(k, 2), lax.rem(k, SLOTS), lax.rem(k, self.states)
            self.cy_hop(k).wait()
            r.c_state[slot] = r.c_state[slot] + r.cy_in[four]
            start_if(self.line_hops(k)[0][1])
            self.ax_hop(k).wait()
            r.ay_out[two] = r.ax_keep[two, 1 - y] + r.ax_in[four, 1 - y]
            self.ay_hop(k).start()
            r.a_sum[lax.rem(k, 4)] = r.ax_keep[two, y] + r.ax_in[four, y]

        stage(2, second)

        def line_step(k, hop):
            name, sends, receives, count = self.line_hops(k)[hop]
            four = lax.rem(k, SLOTS)
            send_wait_if(sends)
            for condition, first in receives:

                @pl.when(condition)
                def _(first=first):
                    sends[0][1].wait_recv()
                    rows = self.c_rows(k, first, count)
                    arrived = (r.ca_in, r.cb_in, r.cc_in)[hop]
                    rows[...] = rows[...] + arrived[four]

            if hop < 2:
                start_if(self.line_hops(k)[hop + 1][1])

        def third(k):
            line_step(k, 0)
            four = lax.rem(k, SLOTS)
            self.ay_hop(k).wait()
            r.a_sum[lax.rem(k, 4)] = r.a_sum[lax.rem(k, 4)] + r.ay_in[four]
            start_if(self.sum_hops(k)[A1])

        stage(3, third)

        def fourth(k):
            line_step(k, 1)
            four, slot = lax.rem(k, SLOTS), lax.rem(k, 4)
            hops = self.sum_hops(k)
            send_wait_if(hops[A1])

            @pl.when((z > 0) & (z < LINE - 1))
            def _():
                hops[A1][0][1].wait_recv()
                r.a_sum[slot] = r.a_sum[slot] + r.a1_in[four]

            start_if(hops[A2])

        stage(4, fourth)

        def fifth(k):
            line_step(k, 2)
            self.cx_hop(k).start()
            four, slot = lax.rem(k, SLOTS), lax.rem(k, 4)
            hops = self.sum_hops(k)
            send_wait_if(hops[A2])

            @pl.when((z > 0) & (z < LINE - 1))
            def _():
                hops[A2][0][1].wait_recv()
                r.a_state[lax.rem(k, self.states_a), x] = r.a_sum[slot] + r.a2_in[four]

            start_if(hops[A3])

        stage(5, fifth)

        def sixth(k):
            four = lax.rem(k, SLOTS)
            hops = self.sum_hops(k)
            send_wait_if(hops[A3])
            pl.when((z == 0) | (z == LINE - 1))(lambda: hops[A3][0][1].wait_recv())
            self.ag_hop(k).start()
            self.cx_hop(k).wait()
            rows = self.c_rows(k, z, 1)
            rows[...] = rows[...] + r.cx_in[four]
            for sends, copy, _ in self.gather_hops(k, 0):
                pl.when(sends)(copy.start)

        stage(6, sixth)

        def gather_step(k, distance):
            for sends, copy, receives in self.gather_hops(k, distance):
                pl.when(sends)(copy.wait_send)
                pl.when(receives)(copy.wait_recv)
            if distance < 2:
                for sends, copy, _ in self.gather_hops(k, distance + 1):
                    pl.when(sends)(copy.start)

        def seventh(k):
            gather_step(k, 0)
            self.ag_hop(k).wait()
            for copy in self.store_a(k):
                copy.start()

        stage(7, seventh)

        def eighth(k):
            gather_step(k, 1)
            for copy in self.store_a(k):
                copy.wait()

        stage(8, eighth)

        def ninth(k):
            gather_step(k, 2)
            for copy in self.store(k):
                copy.start()

        stage(9, ninth)

        def tenth(k):
            for copy in self.store(k):
                copy.wait()

        stage(10, tenth)

    def cy_hop(self, k):
        return self.slotted(CY, k, self.refs.cy_out.at[lax.rem(k, 2)], self.at_y)

    def ax_hop(self, k):
        return self.slotted(AX, k, self.refs.ax_out.at[lax.rem(k, 2)], self.at_x)

    def ay_hop(self, k):
        return self.slotted(AY, k, self.refs.ay_out.at[lax.rem(k, 2)], self.at_y)

    def cx_hop(self, k):
        return self.slotted(CX, k, self.c_rows(k, self.z, 1), self.at_x)

    def ag_hop(self, k):
        final = self.refs.a_state.at[lax.rem(k, self.states_a), self.x]
        return self.copy(AG, k, final, final, self.at_x)


class VectorSum:
    def __init__(self, reducer, value, arrived, send, recv):
        self.value, self.arrived, self.send, self.recv = value, arrived, send, recv
        self.net = reducer

    def hop(self, index, device):
        return pltpu.make_async_remote_copy(
            src_ref=self.value,
            dst_ref=self.arrived.at[index],
            send_sem=self.send.at[index],
            recv_sem=self.recv.at[index],
            device_id=device,
            device_id_type=MESH,
        )

    def exchange(self, index):
        return self.hop(index, (self.net.at_core, self.net.at_y, self.net.at_x)[index])

    def step(self, at):
        z, value, arrived = self.net.z, self.value, self.arrived
        middle = (z > 0) & (z < LINE - 1)
        sends = {
            3: ((z == 0, self.net.at_up), (z == LINE - 1, self.net.at_down)),
            4: ((z == 1, self.net.at_up), (z == 2, self.net.at_down)),
            5: ((z == 1, self.net.at_down), (z == 2, self.net.at_up)),
        }

        def start(index):
            for condition, device in sends[index]:
                pl.when(condition)(self.hop(index, device).start)

        def finish(index, receives, add):
            for condition, device in sends[index]:
                pl.when(condition)(self.hop(index, device).wait_send)

            @pl.when(receives)
            def _():
                self.hop(index, sends[index][0][1]).wait_recv()
                value[...] = arrived[index] + value[...] if add else arrived[index]

        def first():
            self.exchange(0).start()

        def pair(index):
            self.exchange(index).wait()
            value[...] = value[...] + arrived[index]
            if index < 2:
                self.exchange(index + 1).start()
            else:
                start(3)

        def outer():
            finish(3, middle, True)
            start(4)

        def inner():
            finish(4, middle, True)
            start(5)

        pl.when(at == 0)(first)
        for index in range(3):
            pl.when(at == index + 1)(functools.partial(pair, index))
        pl.when(at == 4)(outer)
        pl.when(at == 5)(inner)
        pl.when(at == 6)(lambda: finish(5, (z == 0) | (z == LINE - 1), False))


LANES = 128
PARTS = 4
WIDE = 1152


def gelu_both(u):
    c0, c1 = 0.7978845608028654, 0.044715
    square = u * u
    t = jnp.tanh(c0 * u * (1.0 + c1 * square))
    half = 0.5 + 0.5 * t
    slope = half + (0.5 * c0) * u * (1.0 - t * t) * (1.0 + (3.0 * c1) * square)
    return u * half, slope


def norm_rows(values):
    centred = values - jnp.mean(values, axis=-1, keepdims=True)
    inverse = lax.rsqrt(jnp.mean(centred * centred, axis=-1, keepdims=True) + 1e-05)
    return centred * inverse, inverse


def norm_rows_back(grad_hat, normed, inverse):
    mean_grad = jnp.mean(grad_hat, axis=-1, keepdims=True)
    mean_cross = jnp.mean(grad_hat * normed, axis=-1, keepdims=True)
    return inverse * (grad_hat - mean_grad - normed * mean_cross)


def column_sum(values):
    return jnp.sum(values, axis=0, keepdims=True)


def block(i, count):
    return pl.ds(pl.multiple_of(i * count, count), count)


def identity(size):
    row = lax.broadcasted_iota(jnp.int32, (size, size), 0)
    column = lax.broadcasted_iota(jnp.int32, (size, size), 1)
    return jnp.where(row == column, 1.0, 0.0).astype(BF16)


def turned(eye, rows):
    width = rows.shape[1]
    pieces = []
    for at in range(0, width, LANES):
        size = min(LANES, width - at)
        pieces.append(dot(eye[:size, :size], rows[:, at : at + size], NT))
    return jnp.concatenate(pieces, axis=0)


def leftover_rows(tiles):
    first, second, third = tiles
    return [
        [first[:96]],
        [second[:64], first[96:]],
        [third[:32], second[64:]],
        [third[32:]],
    ]


def layer_kernel(reducer, names, *refs):
    r = types.SimpleNamespace(**dict(zip(names, refs)))
    width, part_rows = r.tokens.shape[1:]
    seq = PARTS * part_rows
    feat, ff = width // PARTS, r.w_up.shape[1] // PARTS
    main = ff // LANES
    left = ff - main * LANES
    stride = (r.w_up.shape[1] // LANES - main) // (PARTS - 1)
    heads, group = width // HD, 4
    reducer.bind(r.parts, r.total, r)
    narrow, y = reducer.narrow, reducer.y
    gain1, bias1, gain2, bias2, bias_down = (
        ref[...].reshape(1, width) for ref in (r.gain1, r.bias1, r.gain2, r.bias2, r.bias_down)
    )
    eye = identity(LANES)
    vec = r.vec
    stage = r.square.at[2]
    vector_sum = VectorSum(reducer, vec, r.vec_in, r.vec_send, r.vec_recv)

    def local(index, source, target):
        return pltpu.make_async_copy(source, target, r.local.at[index])

    def spread(j, source, target):
        remote = [
            pltpu.make_async_remote_copy(
                src_ref=source.at[device[1]],
                dst_ref=target.at[narrow],
                send_sem=r.spread_send.at[j, d],
                recv_sem=r.spread_recv.at[j, d],
                device_id=device,
                device_id_type=MESH,
            )
            for d, device in enumerate((reducer.at_core, reducer.at_y, reducer.at_cross))
        ]
        return remote, local(j, source.at[narrow], target.at[narrow])

    def weights(i, tiles):
        two = lax.rem(i, 2)
        return [
            pltpu.make_async_copy(
                source.at[:, pl.ds(pl.multiple_of(tile * LANES, LANES), LANES)],
                target.at[two, :, pl.ds(q * LANES, LANES)],
                r.w_load.at[two, n, q],
            )
            for n, (source, target) in enumerate(((r.w_up, r.w_up_in), (r.w_down, r.w_down_in)))
            for q, tile in enumerate(tiles)
        ]

    main_tiles = lambda i: [i + stride * q for q in range(PARTS)]
    left_tiles = [main + stride * q for q in range(PARTS - 1)]

    squares = [local(4 + j, r.w_qkv.at[j], r.square.at[j]) for j in range(3)]
    for copy in squares:
        copy.start()
    reducer.barrier()
    tokens, tokens_own = spread(0, r.tokens, r.x_in)
    cots, cots_own = spread(1, r.cot, r.c_in)
    for copy in tokens + [tokens_own]:
        copy.start()
    cots[0].start()
    cots_own.start()
    for copy in weights(0, main_tiles(0)):
        copy.start()
    vec[...] = jnp.zeros_like(vec)
    for target in (r.q, r.k, r.v, r.m, r.g):
        target[:, width:] = jnp.zeros((seq, WIDE - width), BF16)
    r.acc[...] = jnp.zeros_like(r.acc)
    row = lax.broadcasted_iota(jnp.int32, (seq, seq), 0)
    column = lax.broadcasted_iota(jnp.int32, (seq, seq), 1)
    length = r.lengths[narrow]
    r.bias[...] = jnp.where((column <= row) & (column < length), 0.0, -1e30).astype(BF16)
    r.up_bias[...] = r.bias_up[...].reshape(r.up_bias.shape)

    def first_norm(i):
        rows = block(i, part_rows)
        x = dot(eye, r.x_in[i], NT)
        r.x[rows] = x.astype(BF16)
        normed, _ = norm_rows(x)
        r.h[rows] = (normed * gain1 + bias1).astype(BF16)

    def project(side):
        rows = block(side, seq // 2)
        for j, target in enumerate((r.q, r.k, r.v)):
            target[rows, :width] = dot(r.h[rows], r.square[j], NN).astype(BF16)

    tokens_own.wait()
    first_norm(narrow)
    tokens[0].wait()
    first_norm(tokens_peer(reducer, 0))
    for copy in squares:
        copy.wait()
    project(y)
    for d in (1, 2):
        tokens[d].wait_send()
        cots[d].start()
    for d in (1, 2):
        tokens[d].wait_recv()
        first_norm(tokens_peer(reducer, d))
    project(1 - y)
    w_out = local(4, r.w_out, r.square.at[0])
    w_out.start()

    def head_at(h):
        return pl.multiple_of(jnp.minimum(h * HD // LANES * LANES, WIDE - 256), LANES)

    def forward(i, carry):
        pair = [(h, head_at(h)) for h in (2 * i, 2 * i + 1)]
        attend_heads(pair, r.q, r.k, r.v, r.m, r.bias)
        return carry

    lax.fori_loop(0, heads // 2, forward, 0)
    w_out.wait()

    def second_norm(i, carry):
        rows = block(i, part_rows)
        after = r.x[rows].astype(F32) + dot(r.m[rows, :width], r.square[0], NN)
        r.rows[rows] = after
        normed, _ = norm_rows(after)
        r.h[rows] = (normed * gain2 + bias2).astype(BF16)
        return carry

    lax.fori_loop(0, PARTS, second_norm, 0)
    for copy in cots + [cots_own]:
        copy.wait()
    for i in range(PARTS):
        r.grad[block(i, part_rows)] = dot(eye, r.c_in[i], NT).astype(BF16)

    upper = pl.ds(0, seq)
    lower = pl.ds(seq, seq)

    def put(count, base):
        return [
            local(
                8 + q,
                stage.at[pl.ds(2 * LANES * q, count)],
                r.parts.at[q // 2, q % 2, pl.ds(base, count)],
            )
            for q in range(PARTS)
        ]

    def put_block(i):
        return put(2 * LANES, pl.multiple_of(i * 2 * LANES, 2 * LANES))

    def feed_forward(i, tiles):
        two, count = lax.rem(i, 2), LANES * len(tiles)
        up, down = r.w_up_in[two, :, :count], r.w_down_in[two, :, :count]
        at = [pl.ds(pl.multiple_of(tile * LANES, LANES), LANES) for tile in tiles]
        bias = jnp.concatenate([r.up_bias[:, lanes] for lanes in at], axis=1)
        hidden, cot = r.h[...], r.grad[...]
        act, slope = gelu_both(dot(hidden, up, NN) + bias)
        act = act.astype(BF16)
        grad_up = (dot(cot, down, NN) * slope).astype(BF16)
        r.acc[upper, :width] += dot(act, down, NT)
        r.acc[lower, :width] += dot(grad_up, up, NT)
        total = column_sum(grad_up.astype(F32))
        for q, lanes in enumerate(at):
            vec[0:1, lanes] = total[:, LANES * q : LANES * (q + 1)]
        return dot(act, cot, TN).astype(BF16), dot(grad_up, hidden, TN).astype(BF16)

    def ff_block(i, carry):
        for copy in weights(i, main_tiles(i)):
            copy.wait()

        @pl.when(i + 1 < main)
        def _():
            for copy in weights(i + 1, main_tiles(i + 1)):
                copy.start()

        @pl.when(i + 1 == main)
        def _():
            for copy in weights(main, left_tiles):
                copy.start()

        values = feed_forward(i, main_tiles(i))

        @pl.when(i > 1)
        def _():
            for copy in put_block(i - 1):
                copy.wait()

        for j, value in enumerate(values):
            for q in range(PARTS):
                stage[LANES * (2 * q + j) : LANES * (2 * q + j + 1)] = value[
                    LANES * q : LANES * (q + 1)
                ]
        for copy in put_block(i):
            copy.start()
        return carry

    ff_block(0, 0)
    for copy in put_block(0):
        copy.wait()
    reducer.step(jnp.int32(0))

    def ff_step(s, carry):
        lax.fori_loop(2 * s - 1, 2 * s + 1, ff_block, 0)
        reducer.step(s)
        return carry

    ff_steps = main // 2
    lax.fori_loop(1, ff_steps, ff_step, 0)
    lax.fori_loop(main - 1, main, ff_block, 0)
    for copy in weights(main, left_tiles):
        copy.wait()
    values = feed_forward(main, left_tiles)
    for copy in put_block(main - 1):
        copy.wait()
    for j, value in enumerate(values):
        tiles = [value[LANES * q : LANES * (q + 1)] for q in range(PARTS - 1)]
        for q, pieces in enumerate(leftover_rows(tiles)):
            at = 2 * LANES * q + left * j
            for piece in pieces:
                stage[at : at + piece.shape[0]] = piece
                at += piece.shape[0]
    put_left = put(2 * left, 2 * LANES * main)
    for copy in put_left:
        copy.start()
    reducer.step(jnp.int32(ff_steps))
    done = ff_steps + 1
    for copy in put_left:
        copy.wait()

    def add_vector(index, value):
        vec[index : index + 1, :width] = vec[index : index + 1, :width] + value

    def middle_rows(i, carry):
        rows = block(i, part_rows)
        after = r.rows[rows]
        result = r.acc[rows, :width] + after + bias_down
        r.x_in[i] = turned(eye, result.astype(BF16)).astype(BF16)
        normed, inverse = norm_rows(after)
        grad = r.acc[pl.ds(pl.multiple_of(seq + i * part_rows, part_rows), part_rows), :width]
        cot = r.grad[rows].astype(F32)
        add_vector(3, column_sum(grad * normed))
        add_vector(4, column_sum(grad))
        add_vector(5, column_sum(cot))
        grad_after = cot + norm_rows_back(grad * gain2, normed, inverse)
        r.rows[rows] = grad_after
        r.grad[rows] = grad_after.astype(BF16)
        return carry

    lax.fori_loop(0, PARTS, middle_rows, 0)
    four = 4 * HD
    early = []
    for quarter in range(PARTS):
        start = feat * quarter // LANES * LANES
        offset = feat * quarter - start
        product = dot(r.m[:, start : start + 384], r.grad[...], TN)
        for p in range(2):
            at = four * quarter + 2 * HD * p
            first = offset + 2 * HD * p
            stage[at : at + 2 * HD] = product[first : first + 2 * HD].astype(BF16)
        r.acc[HD * quarter : HD * (quarter + 1), :width] = product[
            offset + four : offset + four + HD
        ]
        early.append(
            local(
                8 + quarter,
                stage.at[pl.ds(four * quarter, four)],
                r.parts.at[quarter // 2, quarter % 2, pl.ds(2 * ff, four)],
            )
        )
        early[-1].start()
    r.g[:, :width] = dot(r.grad[...], r.square[0], NT).astype(BF16)
    for copy in early:
        copy.wait()
    w_query = local(4, r.w_qkv.at[0], r.square.at[0])
    w_query.start()
    reducer.step(jnp.int32(done))
    done += 1
    outs, outs_own = spread(2, r.x_in, r.output)
    for copy in outs + [outs_own]:
        copy.start()

    def head_step(s, carry):
        def one(h, carry):
            head_back(h, head_at(h), r.q, r.k, r.v, r.g, r.bias)
            return carry

        lax.fori_loop(s * group, (s + 1) * group, one, 0)
        reducer.step(done + s)
        return carry

    lax.fori_loop(0, heads // group, head_step, 0)
    done += heads // group

    def first_again(i, carry):
        rows = block(i, part_rows)
        normed, _ = norm_rows(r.x[rows].astype(F32))
        r.h[rows] = (normed * gain1 + bias1).astype(BF16)
        return carry

    lax.fori_loop(0, PARTS, first_again, 0)
    sizes = (width - 2 * feat - four, 2 * feat)
    bases = (2 * ff + four, 2 * ff + width - 2 * feat)

    def tail_put(turn):
        pair, quarter = turn // PARTS, turn % PARTS
        return local(
            8 + turn % 2,
            stage.at[pl.ds(2 * feat * (turn % 2), sizes[pair])],
            r.parts.at[quarter // 2, quarter % 2, pl.ds(bases[pair], sizes[pair])],
        )

    for turn in range(2 * PARTS):
        pair, quarter = turn // PARTS, turn % PARTS
        start = feat * quarter // LANES * LANES
        offset = feat * quarter - start
        units = [] if pair else [r.acc[HD * quarter : HD * (quarter + 1), :width]]
        for left_ref, right_ref in ((r.k, r.h), (r.v, r.h)) if pair else ((r.q, r.h),):
            product = dot(left_ref[:, start : start + 384], right_ref[...], TN)
            units += [product[offset + HD * u : offset + HD * (u + 1)] for u in range(5)]
        if turn >= 2 and turn % PARTS >= 2:
            tail_put(turn - 2).wait()
        for p in range(len(units) // 2):
            at = 2 * feat * (turn % 2) + 2 * HD * p
            stage[at : at + 2 * HD] = jnp.concatenate(units[2 * p : 2 * p + 2], axis=0).astype(
                BF16
            )
        tail_put(turn).start()
        if turn % PARTS == PARTS - 1:
            tail_put(turn - 1).wait()
            tail_put(turn).wait()
            reducer.step(jnp.int32(done))
            done += 1
    w_value = local(3, r.w_qkv.at[2], r.square.at[2])
    w_value.start()
    w_query.wait()
    r.acc[upper, :width] = dot(r.q[:, :width], r.square[0], NT)
    r.acc[upper, :width] += dot(r.k[:, :width], r.square[1], NT)
    reducer.step(jnp.int32(done))
    done += 1
    w_value.wait()
    r.acc[upper, :width] += dot(r.v[:, :width], r.square[2], NT)

    def last_norm(i, carry):
        rows = block(i, part_rows)
        normed, inverse = norm_rows(r.x[rows].astype(F32))
        grad = r.acc[rows, :width]
        add_vector(1, column_sum(grad * normed))
        add_vector(2, column_sum(grad))
        back = r.rows[rows] + norm_rows_back(grad * gain1, normed, inverse)
        r.c_in[i] = turned(eye, back.astype(BF16)).astype(BF16)
        return carry

    lax.fori_loop(0, PARTS, last_norm, 0)

    steps = reducer.rounds + 11
    grads, grads_own = spread(3, r.c_in, r.input_grad)
    turn = 32 * narrow
    lane = lax.broadcasted_iota(jnp.int32, (1, LANES), 1)

    def mix(tile, mask, value):
        lanes = pl.ds(pl.multiple_of(tile * LANES, LANES), LANES)
        r.acc[:, lanes] = jnp.where(mask, value, r.acc[:, lanes])

    def settle(j):
        base = pl.multiple_of(j * 2 * LANES, 2 * LANES)
        place = pl.multiple_of(turn + j * LANES, 32)
        get = local(4, r.total.at[pl.ds(base, 2 * LANES)], stage.at[pl.ds(0, 2 * LANES)])
        get.start()
        get.wait()
        give = local(5, stage.at[pl.ds(0, LANES)], r.down.at[pl.ds(place, LANES)])
        give.start()
        value = pltpu.roll(turned(eye, stage[LANES : 2 * LANES]), turn, 1)
        mix(j, lane >= turn, value)
        mix(j + 1, lane < turn, value)
        give.wait()

    def settle_left():
        get = local(4, r.total.at[pl.ds(2 * LANES * main, 2 * left)], stage.at[pl.ds(0, 2 * left)])
        get.start()
        get.wait()
        gives = []
        for piece in range(left // 32):
            place = lax.rem(turn + main * LANES + 32 * piece, ff)
            gives.append(
                local(
                    8 + piece,
                    stage.at[pl.ds(32 * piece, 32)],
                    r.down.at[pl.ds(pl.multiple_of(place, 32), 32)],
                )
            )
            gives[-1].start()
        value = turned(eye, stage[left : left + LANES])
        mix(main, (lane >= turn) & (lane < left), pltpu.roll(value, turn, 1))
        mix(0, lane < turn, pltpu.roll(value, lax.rem(turn + LANES - left, LANES), 1))
        r.square[0] = r.acc[:, :ff].astype(BF16)
        local(6, r.square.at[0], r.up).start()
        for copy in gives:
            copy.wait()

    def drain(t, carry):
        reducer.step(t)

        @pl.when(t == done + 3)
        def _():
            for copy in grads + [grads_own]:
                copy.start()

        vector_sum.step(t - done)
        at = t - done
        for i in range(2):
            pl.when(at < 3)(functools.partial(settle, 2 * at + i))
        pl.when(at == 3)(lambda: settle(6))
        pl.when(at == 5)(lambda: settle(7))
        pl.when(at == 6)(settle_left)
        return carry

    lax.fori_loop(done, steps, drain, 0)
    first = vec[0:1]
    others = vec[:, :WIDE]
    r.share[...] = pltpu.roll(others, lax.rem(WIDE - feat * narrow, WIDE), 1)
    hidden = PARTS * ff
    r.share[0:1, :ff] = pltpu.roll(first, lax.rem(hidden - ff * narrow, hidden), 1)[:, :ff]
    finish = local(7, r.share, r.vector)
    finish.start()
    for copy in outs + [outs_own] + grads + [grads_own]:
        copy.wait()
    local(6, r.square.at[0], r.up).wait()
    finish.wait()


def tokens_peer(reducer, d):
    return (reducer.at_core, reducer.at_y, reducer.at_cross)[d][1]


def softmax_parts(scores):
    expo = jnp.exp(scores - jnp.max(scores, axis=1, keepdims=True))
    return expo * (1.0 / jnp.sum(expo, axis=1, keepdims=True))


def attend_heads(pair, q_ref, k_ref, v_ref, out_ref, bias_ref):
    half = q_ref.shape[0] // 2
    results = []
    for h, start in pair:
        window = pl.ds(start, 256)
        mask = head_mask(h, start, 256)
        query = jnp.where(mask, q_ref[:, window], 0)
        keys, values = k_ref[:, window], v_ref[:, window]
        for part in range(2):
            count = (part + 1) * half
            rows = slice(part * half, count)
            scores = dot(query[rows], keys[:count], NT) * SCALE + bias_ref[rows, :count]
            probs = softmax_parts(scores).astype(BF16)
            mixed = dot(probs, values[:count], NN).astype(BF16)
            results.append((rows, window, mask, mixed))
    for rows, window, mask, mixed in results:
        out_ref[rows, window] = jnp.where(mask, mixed, out_ref[rows, window])


def head_back(h, start, q_ref, k_ref, v_ref, grad_ref, bias_ref):
    half = q_ref.shape[0] // 2
    window = pl.ds(start, 256)
    mask = head_mask(h, start, 256)
    query = jnp.where(mask, q_ref[:, window], 0)
    grad = jnp.where(mask, grad_ref[:, window], 0)
    keys, values = k_ref[:, window], v_ref[:, window]
    grads = []
    for part in range(2):
        count = (part + 1) * half
        rows = slice(part * half, count)
        scores = dot(query[rows], keys[:count], NT) * SCALE + bias_ref[rows, :count]
        grad_probs = dot(grad[rows], values[:count], NT)
        probs = softmax_parts(scores)
        inner = jnp.sum(probs * grad_probs, axis=1, keepdims=True)
        grad_scores = (probs * (grad_probs - inner) * SCALE).astype(BF16)
        gq = dot(grad_scores, keys[:count], NN).astype(BF16)
        gk = dot(grad_scores, query[rows], TN)
        gv = dot(probs.astype(BF16), grad[rows], TN)
        grads.append((gq, gk, gv))
    (gq0, gk0, gv0), (gq1, gk1, gv1) = grads
    q_ref[:half, window] = jnp.where(mask, gq0, q_ref[:half, window])
    q_ref[half:, window] = jnp.where(mask, gq1, q_ref[half:, window])
    for ref, first, second in ((k_ref, gk0, gk1), (v_ref, gv0, gv1)):
        top, bottom = (first + second[:half]).astype(BF16), second[half:].astype(BF16)
        ref[:half, window] = jnp.where(mask, top, ref[:half, window])
        ref[half:, window] = jnp.where(mask, bottom, ref[half:, window])


def whole_layer(**arrays):
    parts, width, part_rows = arrays["tokens"].shape
    seq, hidden = parts * part_rows, arrays["w_up"].shape[1]
    ff = hidden // parts
    rows = 2 * ff + width
    reducer = Reducer(128, 96, width, rows)
    scratch = reducer.scratch()
    low = lambda *shape: pltpu.VMEM(shape, BF16)
    full = lambda *shape: pltpu.VMEM(shape, F32)
    dma = lambda *shape: pltpu.SemaphoreType.DMA(shape)
    scratch.update(
        x_in=low(parts, width, part_rows),
        c_in=low(parts, width, part_rows),
        w_up_in=low(2, width, parts * LANES),
        w_down_in=low(2, width, parts * LANES),
        square=low(3, width, width),
        q=low(seq, WIDE),
        k=low(seq, WIDE),
        v=low(seq, WIDE),
        m=low(seq, WIDE),
        g=low(seq, WIDE),
        h=low(seq, width),
        grad=low(seq, width),
        x=low(seq, width),
        rows=full(seq, width),
        acc=full(width, WIDE),
        bias=low(seq, seq),
        up_bias=full(1, hidden),
        vec=full(8, hidden),
        vec_in=full(6, 8, hidden),
        share=full(8, WIDE),
        vec_send=dma(6),
        vec_recv=dma(6),
        local=dma(12),
        w_load=dma(2, 2, parts),
        spread_send=dma(4, 3),
        spread_recv=dma(4, 3),
    )
    hbm = pl.BlockSpec(memory_space=pl.ANY)
    vmem = pl.BlockSpec(memory_space=pltpu.VMEM)
    low_out = lambda *shape: jax.ShapeDtypeStruct(shape, BF16)
    outputs = dict(
        parts=low_out(2, parts // 2, rows, width),
        total=low_out(rows, width),
        down=low_out(ff, width),
        up=low_out(width, ff),
        output=low_out(parts, width, part_rows),
        input_grad=low_out(parts, width, part_rows),
        vector=jax.ShapeDtypeStruct((8, WIDE), F32),
    )
    smem = pl.BlockSpec(memory_space=pltpu.SMEM)
    names = list(arrays) + list(outputs) + list(scratch)
    results = pl.pallas_call(
        functools.partial(layer_kernel, reducer, names),
        out_shape=tuple(outputs.values()),
        in_specs=[hbm] * 6 + [smem] + [vmem] * (len(arrays) - 7),
        out_specs=[hbm] * len(outputs),
        scratch_shapes=list(scratch.values()),
        compiler_params=pltpu.CompilerParams(
            collective_id=0, has_side_effects=True, vmem_limit_bytes=VMEM_LIMIT
        ),
        name="whole_layer",
    )(*arrays.values())
    return types.SimpleNamespace(**dict(zip(outputs, results)))


def finish_kernel(names, *refs):
    r = types.SimpleNamespace(**dict(zip(names, refs)))
    rows, step = r.down.shape[0], 112
    feat = r.out.shape[0]

    def copy(index, source, target):
        return pltpu.make_async_copy(source, target, r.moves.at[index])

    loads = [
        copy(0, r.down, r.down_in),
        copy(1, r.up, r.up_in),
        copy(2, r.total.at[pl.ds(r.total.shape[0] - rows, rows)], r.rest_in),
        copy(3, r.grad, r.grad_in),
    ]
    plain = copy(4, r.output, r.output_in)
    for move in loads + [plain]:
        move.start()
    stores = []

    def store(source, target):
        stores.append(copy(5 + len(stores), source, target))
        stores[-1].start()

    r.up_bias_to[...] = r.vector[0, :rows]
    for index, target in enumerate((r.gain1, r.bias1, r.gain2, r.bias2, r.down_bias)):
        target[...] = r.vector[index + 1, :feat]
    wides = ((r.down_in, r.down_wide, r.down_to), (r.up_in, r.up_wide, r.up_to))
    for load, (source, wide, target) in zip(loads, wides):
        load.wait()
        for at in range(0, rows, step):
            wide[at : at + step] = source[at : at + step].astype(F32)
            if (at // step) % 2:
                area = pl.ds(at - step, 2 * step)
                store(wide.at[area], target.at[area])
    loads[2].wait()
    sent = 0
    for at in range(0, rows, step):
        r.rest_wide[at : at + step] = r.rest_in[at : at + step].astype(F32)
        while sent < rows and at + step >= sent + feat:
            area = pl.ds(sent, feat)
            target = r.out if sent == 0 else r.qkv.at[pl.ds(sent - feat, feat)]
            store(r.rest_wide.at[area], target)
            sent += feat
    loads[3].wait()
    for i in range(r.grad_in.shape[0]):
        r.grad_wide[i] = r.grad_in[i].astype(F32)
        store(r.grad_wide.at[i], r.grad_to.at[i])
    plain.wait()
    store(r.output_in, r.result)
    for move in stores:
        move.wait()


def finish(**arrays):
    shape = {name: array.shape for name, array in arrays.items()}
    rows, width = shape["down"]
    feat = width // PARTS
    wide = lambda *size: jax.ShapeDtypeStruct(size, F32)
    outputs = dict(
        result=jax.ShapeDtypeStruct(shape["output"], BF16),
        grad_to=wide(*shape["grad"]),
        qkv=wide(3 * feat, width),
        out=wide(feat, width),
        up_to=wide(*shape["up"]),
        down_to=wide(rows, width),
        gain1=wide(feat),
        bias1=wide(feat),
        gain2=wide(feat),
        bias2=wide(feat),
        up_bias_to=wide(rows),
        down_bias=wide(feat),
    )
    kept = lambda name: pltpu.VMEM(shape[name], arrays[name].dtype)
    square = lambda dtype: pltpu.VMEM((rows, width), dtype)
    scratch = dict(
        down_in=kept("down"),
        up_in=kept("up"),
        rest_in=square(arrays["total"].dtype),
        grad_in=kept("grad"),
        output_in=kept("output"),
        down_wide=square(F32),
        up_wide=square(F32),
        rest_wide=square(F32),
        grad_wide=pltpu.VMEM(shape["grad"], F32),
        moves=pltpu.SemaphoreType.DMA((32,)),
    )
    hbm = pl.BlockSpec(memory_space=pl.ANY)
    vmem = pl.BlockSpec(memory_space=pltpu.VMEM)
    names = list(arrays) + list(outputs) + list(scratch)
    results = pl.pallas_call(
        functools.partial(finish_kernel, names),
        out_shape=tuple(outputs.values()),
        in_specs=[hbm] * (len(arrays) - 1) + [vmem],
        out_specs=[hbm] * 6 + [vmem] * 6,
        scratch_shapes=list(scratch.values()),
        compiler_params=pltpu.CompilerParams(vmem_limit_bytes=VMEM_LIMIT),
        name="finish",
    )(*arrays.values())
    return types.SimpleNamespace(**dict(zip(outputs, results)))


def on_device(
    wide,
    tokens,
    lengths,
    norm1_gain,
    norm1_bias,
    w_qkv,
    w_out,
    norm2_gain,
    norm2_bias,
    w_up,
    bias_up,
    w_down,
    bias_down,
    cotangent,
):
    width = w_out.shape[0]
    feat = width // tokens.shape[0]
    got = whole_layer(
        tokens=tokens.transpose(0, 2, 1),
        cot=cotangent.transpose(0, 2, 1),
        w_qkv=w_qkv.transpose(1, 0, 2),
        w_out=w_out,
        w_up=w_up,
        w_down=w_down.T,
        lengths=lengths,
        gain1=norm1_gain,
        bias1=norm1_bias,
        gain2=norm2_gain,
        bias2=norm2_bias,
        bias_up=bias_up,
        bias_down=bias_down,
    )
    if wide > BLOCK:
        groups = [list(range(i, wide, BLOCK)) for i in range(BLOCK)]
        got.total, got.down, got.up, got.vector = (
            lax.psum(a.astype(F32), "wide", axis_index_groups=groups)
            for a in (got.total, got.down, got.up, got.vector)
        )
    last = finish(
        output=got.output,
        grad=got.input_grad,
        total=got.total,
        down=got.down,
        up=got.up,
        vector=got.vector,
    )
    return (
        last.result.transpose(0, 2, 1),
        last.grad_to.transpose(0, 2, 1),
        last.gain1,
        last.bias1,
        last.qkv.reshape(3, feat, width).transpose(2, 0, 1),
        last.out,
        last.gain2,
        last.bias2,
        last.up_to,
        last.up_bias_to,
        last.down_to,
        last.down_bias,
    )


def solution(mesh):
    rows = P("wide", "narrow", None)
    in_specs = (rows, P("wide")) + (P(),) * 10 + (rows,)
    out_specs = (
        rows,
        rows,
        P("narrow"),
        P("narrow"),
        P(None, None, "narrow"),
        P("narrow", None),
        P("narrow"),
        P("narrow"),
        P(None, "narrow"),
        P("narrow"),
        P("narrow", None),
        P("narrow"),
    )
    return jax.shard_map(
        functools.partial(on_device, mesh.shape["wide"]),
        mesh=mesh,
        in_specs=in_specs,
        out_specs=out_specs,
        check_vma=False,
    )
```

```python
import functools
import types

import jax
import jax.numpy as jnp
from jax import lax
from jax.experimental import pallas as pl
from jax.experimental.pallas import tpu as pltpu
from jax.sharding import PartitionSpec as P

HD = 56
SCALE = HD**-0.5
F32, BF16 = jnp.float32, jnp.bfloat16
MESH = pl.DeviceIdType.MESH
VMEM_LIMIT = 62 * 1024 * 1024
LINE, PAIR = 4, 2
BLOCK = LINE * PAIR
SLOTS = 4
CORE, CY, CA, CB, CC, CX, AX, AY, A1, A2, A3, AG, GATHER = range(13)
CHANNELS = GATHER + 6


def dot(a, b, dims):
    return lax.dot_general(a, b, (dims, ((), ())), preferred_element_type=F32)


NN, NT, TN = ((1,), (0,)), ((1,), (1,)), ((0,), (0,))


def head_mask(h, start, size):
    lane = start + lax.broadcasted_iota(jnp.int32, (1, size), 1)
    return (lane >= h * HD) & (lane < h * HD + HD)


class Reducer:
    hops = 9

    def __init__(self, rows_c, rows_a, width, total):
        self.rounds = total // (rows_c + rows_a)
        self.states, self.states_a = 10, 8
        self.rows_c, self.rows_a, self.width = rows_c, rows_a, width
        self.rows = rows_c + rows_a
        self.shard, self.half = rows_c // LINE, rows_a // 2

    def scratch(self):
        c, a, q, h, d = self.rows_c, self.rows_a, self.shard, self.half, self.width
        buffers = dict(
            own=(2, self.rows, d),
            core_in=(2, 2, self.rows, d),
            cy_out=(2, c, d),
            cy_in=(SLOTS, c, d),
            c_state=(self.states, c, d),
            ca_in=(SLOTS, 3 * q, d),
            cb_in=(SLOTS, 2 * q, d),
            cc_in=(SLOTS, q, d),
            cx_in=(SLOTS, q, d),
            ax_out=(2, 2, h, d),
            ax_keep=(2, 2, h, d),
            ax_in=(SLOTS, 2, h, d),
            ay_out=(2, h, d),
            ay_in=(SLOTS, h, d),
            a_sum=(4, h, d),
            a1_in=(SLOTS, h, d),
            a2_in=(SLOTS, h, d),
            a_state=(self.states_a, 2, h, d),
        )
        result = {name: pltpu.VMEM(shape, BF16) for name, shape in buffers.items()}
        result.update(
            net_send=pltpu.SemaphoreType.DMA((CHANNELS, SLOTS)),
            net_recv=pltpu.SemaphoreType.DMA((CHANNELS, SLOTS)),
            load=pltpu.SemaphoreType.DMA((2,)),
            c_store=pltpu.SemaphoreType.DMA((2,)),
            a_store=pltpu.SemaphoreType.DMA((2,)),
        )
        return result

    def bind(self, part_ref, out_ref, refs):
        self.part_ref, self.out_ref, self.refs = part_ref, out_ref, refs
        wide, narrow = lax.axis_index("wide"), lax.axis_index("narrow")
        self.wide, self.narrow = wide, narrow
        self.z, self.x = lax.rem(wide, BLOCK) // PAIR, lax.rem(wide, PAIR)
        self.y, self.core = narrow // 2, lax.rem(narrow, 2)
        flip = lambda index, bit: index + 1 - 2 * bit
        self.at_core = (wide, flip(narrow, self.core))
        self.at_y = (wide, narrow + 2 - 4 * self.y)
        self.at_cross = (wide, flip(narrow, self.core) + 2 - 4 * self.y)
        self.at_x = (flip(wide, self.x), narrow)
        self.at_up = (wide + PAIR, narrow)
        self.at_down = (wide - PAIR, narrow)

    def barrier(self):
        z = self.z
        barrier = pltpu.get_barrier_semaphore()

        def greet(target):
            pl.semaphore_signal(barrier, inc=1, device_id=target, device_id_type=MESH)

        for target in (self.at_core, self.at_y, self.at_cross, self.at_x):
            greet(target)
        pl.when(z < LINE - 1)(lambda: greet(self.at_up))
        pl.when(z > 0)(lambda: greet(self.at_down))
        edge = (z == 0) | (z == LINE - 1)
        pl.when(edge)(lambda: pl.semaphore_wait(barrier, 5))
        pl.when(~edge)(lambda: pl.semaphore_wait(barrier, 6))

    def copy(self, channel, k, source, target, device):
        slot = lax.rem(k, SLOTS)
        return pltpu.make_async_remote_copy(
            src_ref=source,
            dst_ref=target,
            send_sem=self.refs.net_send.at[channel, slot],
            recv_sem=self.refs.net_recv.at[channel, slot],
            device_id=device,
            device_id_type=MESH,
        )


    def load(self, k):
        r = self.refs
        return pltpu.make_async_copy(
            self.part_ref.at[:, self.core, pl.ds(k * self.rows, self.rows)],
            r.own,
            r.load.at[lax.rem(k, 2)],
        )

    def core_hop(self, k):
        return self.copy(
            CORE,
            k,
            self.part_ref.at[:, 1 - self.core, pl.ds(k * self.rows, self.rows)],
            self.refs.core_in.at[lax.rem(k, 2)],
            self.at_core,
        )

    def slotted(self, channel, k, source, device):
        r = self.refs
        arrivals = {CY: r.cy_in, CA: r.ca_in, CB: r.cb_in, CC: r.cc_in, CX: r.cx_in}
        arrivals.update({AX: r.ax_in, AY: r.ay_in, A1: r.a1_in, A2: r.a2_in})
        return self.copy(channel, k, source, arrivals[channel].at[lax.rem(k, SLOTS)], device)

    def c_rows(self, k, first, count):
        return self.refs.c_state.at[
            lax.rem(k, self.states), pl.ds(pl.multiple_of(first * self.shard, self.shard), count * self.shard)
        ]

    def line_hops(self, k):
        z, up, down = self.z, self.at_up, self.at_down
        hops = []
        for name, count, up_from in ((CA, 3, 0), (CB, 2, 1), (CC, 1, 2)):
            down_from = LINE - 1 - up_from
            hops.append(
                (
                    name,
                    [
                        (z == up_from, self.slotted(name, k, self.c_rows(k, LINE - count, count), up)),
                        (z == down_from, self.slotted(name, k, self.c_rows(k, 0, count), down)),
                    ],
                    [(z == up_from + 1, LINE - count), (z == down_from - 1, 0)],
                    count,
                )
            )
        return hops

    def gather_hops(self, k, distance):
        z = self.z
        channel = GATHER + 2 * distance
        low, high = jnp.maximum(z - distance, 0), jnp.minimum(z + distance, LINE - 1)
        return [
            (
                (z >= distance) & (z < LINE - 1),
                self.copy(channel, k, self.c_rows(k, low, 1), self.c_rows(k, low, 1), self.at_up),
                z >= distance + 1,
            ),
            (
                (z <= LINE - 1 - distance) & (z > 0),
                self.copy(channel + 1, k, self.c_rows(k, high, 1), self.c_rows(k, high, 1), self.at_down),
                z <= LINE - 2 - distance,
            ),
        ]

    def sum_hops(self, k):
        z, slot = self.z, lax.rem(k, 4)
        own = self.refs.a_sum.at[slot]
        final = self.refs.a_state.at[lax.rem(k, self.states_a), self.x]
        return {
            A1: [
                (z == 0, self.slotted(A1, k, own, self.at_up)),
                (z == LINE - 1, self.slotted(A1, k, own, self.at_down)),
            ],
            A2: [
                (z == 1, self.slotted(A2, k, own, self.at_up)),
                (z == 2, self.slotted(A2, k, own, self.at_down)),
            ],
            A3: [
                (z == 1, self.copy(A3, k, final, final, self.at_down)),
                (z == 2, self.copy(A3, k, final, final, self.at_up)),
            ],
        }

    def store(self, k):
        r, slot, two = self.refs, lax.rem(k, self.states), lax.rem(k, 2)
        base = k * self.rows
        yield pltpu.make_async_copy(
            r.c_state.at[slot], self.out_ref.at[pl.ds(base, self.rows_c)], r.c_store.at[two]
        )

    def store_a(self, k):
        r, slot, two = self.refs, lax.rem(k, self.states_a), lax.rem(k, 2)
        base = k * self.rows + self.rows_c
        for i in range(2):
            yield pltpu.make_async_copy(
                r.a_state.at[slot, i],
                self.out_ref.at[pl.ds(base + i * self.half, self.half)],
                r.a_store.at[two],
            )

    def step(self, t):
        r, c, h, q = self.refs, self.rows_c, self.half, self.shard
        x, y, z = self.x, self.y, self.z

        def stage(delay, body):
            k = t - delay
            pl.when((k >= 0) & (k < self.rounds))(lambda: body(k))

        def start_if(pairs):
            for condition, copy in pairs:
                pl.when(condition)(copy.start)

        def send_wait_if(pairs):
            for condition, copy in pairs:
                pl.when(condition)(copy.wait_send)

        def begin(k):
            self.core_hop(k).start()
            pl.when(k == 0)(self.load(k).start)


        def after_core(k):
            two, four = lax.rem(k, 2), lax.rem(k, SLOTS)
            copy = self.core_hop(k)
            copy.wait()
            self.load(k).wait()
            total = lambda i, rows: r.own[i, rows] + r.core_in[two, i, rows]
            everything = pl.ds(0, c)
            r.cy_out[two] = total(1 - y, everything)
            self.cy_hop(k).start()
            for i in range(2):
                rows = pl.ds(pl.multiple_of(c + (1 - x) * h, 16), h)
                r.ax_out[two, i] = total(i, rows)
            self.ax_hop(k).start()
            r.c_state[lax.rem(k, self.states), :] = total(y, everything)
            for i in range(2):
                rows = pl.ds(pl.multiple_of(c + x * h, 16), h)
                r.ax_keep[two, i] = total(i, rows)
            pl.when(k + 1 < self.rounds)(lambda: self.load(k + 1).start())

        stage(1, after_core)
        stage(0, begin)

        def second(k):
            two, four, slot = lax.rem(k, 2), lax.rem(k, SLOTS), lax.rem(k, self.states)
            self.cy_hop(k).wait()
            r.c_state[slot] = r.c_state[slot] + r.cy_in[four]
            start_if(self.line_hops(k)[0][1])
            self.ax_hop(k).wait()
            r.ay_out[two] = r.ax_keep[two, 1 - y] + r.ax_in[four, 1 - y]
            self.ay_hop(k).start()
            r.a_sum[lax.rem(k, 4)] = r.ax_keep[two, y] + r.ax_in[four, y]

        stage(2, second)

        def line_step(k, hop):
            name, sends, receives, count = self.line_hops(k)[hop]
            four = lax.rem(k, SLOTS)
            send_wait_if(sends)
            for condition, first in receives:

                @pl.when(condition)
                def _(first=first):
                    sends[0][1].wait_recv()
                    rows = self.c_rows(k, first, count)
                    arrived = (r.ca_in, r.cb_in, r.cc_in)[hop]
                    rows[...] = rows[...] + arrived[four]

            if hop < 2:
                start_if(self.line_hops(k)[hop + 1][1])

        def third(k):
            line_step(k, 0)
            four = lax.rem(k, SLOTS)
            self.ay_hop(k).wait()
            r.a_sum[lax.rem(k, 4)] = r.a_sum[lax.rem(k, 4)] + r.ay_in[four]
            start_if(self.sum_hops(k)[A1])

        stage(3, third)

        def fourth(k):
            line_step(k, 1)
            four, slot = lax.rem(k, SLOTS), lax.rem(k, 4)
            hops = self.sum_hops(k)
            send_wait_if(hops[A1])

            @pl.when((z > 0) & (z < LINE - 1))
            def _():
                hops[A1][0][1].wait_recv()
                r.a_sum[slot] = r.a_sum[slot] + r.a1_in[four]

            start_if(hops[A2])

        stage(4, fourth)

        def fifth(k):
            line_step(k, 2)
            self.cx_hop(k).start()
            four, slot = lax.rem(k, SLOTS), lax.rem(k, 4)
            hops = self.sum_hops(k)
            send_wait_if(hops[A2])

            @pl.when((z > 0) & (z < LINE - 1))
            def _():
                hops[A2][0][1].wait_recv()
                r.a_state[lax.rem(k, self.states_a), x] = r.a_sum[slot] + r.a2_in[four]

            start_if(hops[A3])

        stage(5, fifth)

        def sixth(k):
            four = lax.rem(k, SLOTS)
            hops = self.sum_hops(k)
            send_wait_if(hops[A3])
            pl.when((z == 0) | (z == LINE - 1))(lambda: hops[A3][0][1].wait_recv())
            self.ag_hop(k).start()
            self.cx_hop(k).wait()
            rows = self.c_rows(k, z, 1)
            rows[...] = rows[...] + r.cx_in[four]
            for sends, copy, _ in self.gather_hops(k, 0):
                pl.when(sends)(copy.start)

        stage(6, sixth)

        def gather_step(k, distance):
            for sends, copy, receives in self.gather_hops(k, distance):
                pl.when(sends)(copy.wait_send)
                pl.when(receives)(copy.wait_recv)
            if distance < 2:
                for sends, copy, _ in self.gather_hops(k, distance + 1):
                    pl.when(sends)(copy.start)

        def seventh(k):
            gather_step(k, 0)
            self.ag_hop(k).wait()
            for copy in self.store_a(k):
                copy.start()

        stage(7, seventh)

        def eighth(k):
            gather_step(k, 1)
            for copy in self.store_a(k):
                copy.wait()

        stage(8, eighth)

        def ninth(k):
            gather_step(k, 2)
            for copy in self.store(k):
                copy.start()

        stage(9, ninth)

        def tenth(k):
            for copy in self.store(k):
                copy.wait()

        stage(10, tenth)

    def cy_hop(self, k):
        return self.slotted(CY, k, self.refs.cy_out.at[lax.rem(k, 2)], self.at_y)

    def ax_hop(self, k):
        return self.slotted(AX, k, self.refs.ax_out.at[lax.rem(k, 2)], self.at_x)

    def ay_hop(self, k):
        return self.slotted(AY, k, self.refs.ay_out.at[lax.rem(k, 2)], self.at_y)

    def cx_hop(self, k):
        return self.slotted(CX, k, self.c_rows(k, self.z, 1), self.at_x)

    def ag_hop(self, k):
        final = self.refs.a_state.at[lax.rem(k, self.states_a), self.x]
        return self.copy(AG, k, final, final, self.at_x)


class VectorSum:
    def __init__(self, reducer, value, arrived, send, recv):
        self.value, self.arrived, self.send, self.recv = value, arrived, send, recv
        self.net = reducer

    def hop(self, index, device):
        return pltpu.make_async_remote_copy(
            src_ref=self.value,
            dst_ref=self.arrived.at[index],
            send_sem=self.send.at[index],
            recv_sem=self.recv.at[index],
            device_id=device,
            device_id_type=MESH,
        )

    def exchange(self, index):
        return self.hop(index, (self.net.at_core, self.net.at_y, self.net.at_x)[index])

    def step(self, at):
        z, value, arrived = self.net.z, self.value, self.arrived
        middle = (z > 0) & (z < LINE - 1)
        sends = {
            3: ((z == 0, self.net.at_up), (z == LINE - 1, self.net.at_down)),
            4: ((z == 1, self.net.at_up), (z == 2, self.net.at_down)),
            5: ((z == 1, self.net.at_down), (z == 2, self.net.at_up)),
        }

        def start(index):
            for condition, device in sends[index]:
                pl.when(condition)(self.hop(index, device).start)

        def finish(index, receives, add):
            for condition, device in sends[index]:
                pl.when(condition)(self.hop(index, device).wait_send)

            @pl.when(receives)
            def _():
                self.hop(index, sends[index][0][1]).wait_recv()
                value[...] = arrived[index] + value[...] if add else arrived[index]

        def first():
            self.exchange(0).start()

        def pair(index):
            self.exchange(index).wait()
            value[...] = value[...] + arrived[index]
            if index < 2:
                self.exchange(index + 1).start()
            else:
                start(3)

        def outer():
            finish(3, middle, True)
            start(4)

        def inner():
            finish(4, middle, True)
            start(5)

        pl.when(at == 0)(first)
        for index in range(3):
            pl.when(at == index + 1)(functools.partial(pair, index))
        pl.when(at == 4)(outer)
        pl.when(at == 5)(inner)
        pl.when(at == 6)(lambda: finish(5, (z == 0) | (z == LINE - 1), False))


LANES = 128
PARTS = 4
WIDE = 1152


def gelu_both(u):
    c0, c1 = 0.7978845608028654, 0.044715
    square = u * u
    t = jnp.tanh(c0 * u * (1.0 + c1 * square))
    half = 0.5 + 0.5 * t
    slope = half + (0.5 * c0) * u * (1.0 - t * t) * (1.0 + (3.0 * c1) * square)
    return u * half, slope


def norm_rows(values):
    centred = values - jnp.mean(values, axis=-1, keepdims=True)
    inverse = lax.rsqrt(jnp.mean(centred * centred, axis=-1, keepdims=True) + 1e-05)
    return centred * inverse, inverse


def norm_rows_back(grad_hat, normed, inverse):
    mean_grad = jnp.mean(grad_hat, axis=-1, keepdims=True)
    mean_cross = jnp.mean(grad_hat * normed, axis=-1, keepdims=True)
    return inverse * (grad_hat - mean_grad - normed * mean_cross)


def column_sum(values):
    return jnp.sum(values, axis=0, keepdims=True)


def block(i, count):
    return pl.ds(pl.multiple_of(i * count, count), count)


def identity(size):
    row = lax.broadcasted_iota(jnp.int32, (size, size), 0)
    column = lax.broadcasted_iota(jnp.int32, (size, size), 1)
    return jnp.where(row == column, 1.0, 0.0).astype(BF16)


def turned(eye, rows):
    width = rows.shape[1]
    pieces = []
    for at in range(0, width, LANES):
        size = min(LANES, width - at)
        pieces.append(dot(eye[:size, :size], rows[:, at : at + size], NT))
    return jnp.concatenate(pieces, axis=0)


def leftover_rows(tiles):
    first, second, third = tiles
    return [
        [first[:96]],
        [second[:64], first[96:]],
        [third[:32], second[64:]],
        [third[32:]],
    ]


def layer_kernel(reducer, names, *refs):
    r = types.SimpleNamespace(**dict(zip(names, refs)))
    width, part_rows = r.tokens.shape[1:]
    seq = PARTS * part_rows
    feat, ff = width // PARTS, r.w_up.shape[1] // PARTS
    main = ff // LANES
    left = ff - main * LANES
    stride = (r.w_up.shape[1] // LANES - main) // (PARTS - 1)
    heads, group = width // HD, 4
    reducer.bind(r.parts, r.total, r)
    narrow, y = reducer.narrow, reducer.y
    gain1, bias1, gain2, bias2, bias_down = (
        ref[...].reshape(1, width) for ref in (r.gain1, r.bias1, r.gain2, r.bias2, r.bias_down)
    )
    eye = identity(LANES)
    vec = r.vec
    stage = r.square.at[2]
    vector_sum = VectorSum(reducer, vec, r.vec_in, r.vec_send, r.vec_recv)

    def local(index, source, target):
        return pltpu.make_async_copy(source, target, r.local.at[index])

    def spread(j, source, target):
        remote = [
            pltpu.make_async_remote_copy(
                src_ref=source.at[device[1]],
                dst_ref=target.at[narrow],
                send_sem=r.spread_send.at[j, d],
                recv_sem=r.spread_recv.at[j, d],
                device_id=device,
                device_id_type=MESH,
            )
            for d, device in enumerate((reducer.at_core, reducer.at_y, reducer.at_cross))
        ]
        return remote, local(j, source.at[narrow], target.at[narrow])

    def weights(i, tiles):
        two = lax.rem(i, 2)
        return [
            pltpu.make_async_copy(
                source.at[:, pl.ds(pl.multiple_of(tile * LANES, LANES), LANES)],
                target.at[two, :, pl.ds(q * LANES, LANES)],
                r.w_load.at[two, n, q],
            )
            for n, (source, target) in enumerate(((r.w_up, r.w_up_in), (r.w_down, r.w_down_in)))
            for q, tile in enumerate(tiles)
        ]

    main_tiles = lambda i: [i + stride * q for q in range(PARTS)]
    left_tiles = [main + stride * q for q in range(PARTS - 1)]

    squares = [local(4 + j, r.w_qkv.at[j], r.square.at[j]) for j in range(3)]
    for copy in squares:
        copy.start()
    reducer.barrier()
    tokens, tokens_own = spread(0, r.tokens, r.x_in)
    cots, cots_own = spread(1, r.cot, r.c_in)
    for copy in tokens + [tokens_own]:
        copy.start()
    cots[0].start()
    cots_own.start()
    for copy in weights(0, main_tiles(0)):
        copy.start()
    vec[...] = jnp.zeros_like(vec)
    for target in (r.q, r.k, r.v, r.m, r.g):
        target[:, width:] = jnp.zeros((seq, WIDE - width), BF16)
    r.acc[...] = jnp.zeros_like(r.acc)
    row = lax.broadcasted_iota(jnp.int32, (seq, seq), 0)
    column = lax.broadcasted_iota(jnp.int32, (seq, seq), 1)
    length = r.lengths[narrow]
    r.bias[...] = jnp.where((column <= row) & (column < length), 0.0, -1e30).astype(BF16)
    r.up_bias[...] = r.bias_up[...].reshape(r.up_bias.shape)

    def first_norm(i):
        rows = block(i, part_rows)
        x = dot(eye, r.x_in[i], NT)
        r.x[rows] = x.astype(BF16)
        normed, _ = norm_rows(x)
        r.h[rows] = (normed * gain1 + bias1).astype(BF16)

    def project(side):
        rows = block(side, seq // 2)
        for j, target in enumerate((r.q, r.k, r.v)):
            target[rows, :width] = dot(r.h[rows], r.square[j], NN).astype(BF16)

    tokens_own.wait()
    first_norm(narrow)
    tokens[0].wait()
    first_norm(tokens_peer(reducer, 0))
    for copy in squares:
        copy.wait()
    project(y)
    for d in (1, 2):
        tokens[d].wait_send()
        cots[d].start()
    for d in (1, 2):
        tokens[d].wait_recv()
        first_norm(tokens_peer(reducer, d))
    project(1 - y)
    w_out = local(4, r.w_out, r.square.at[0])
    w_out.start()

    def head_at(h):
        return pl.multiple_of(jnp.minimum(h * HD // LANES * LANES, WIDE - 256), LANES)

    def forward(i, carry):
        pair = [(h, head_at(h)) for h in (2 * i, 2 * i + 1)]
        attend_heads(pair, r.q, r.k, r.v, r.m, r.bias)
        return carry

    lax.fori_loop(0, heads // 2, forward, 0)
    w_out.wait()

    def second_norm(i, carry):
        rows = block(i, part_rows)
        after = r.x[rows].astype(F32) + dot(r.m[rows, :width], r.square[0], NN)
        r.rows[rows] = after
        normed, _ = norm_rows(after)
        r.h[rows] = (normed * gain2 + bias2).astype(BF16)
        return carry

    lax.fori_loop(0, PARTS, second_norm, 0)
    for copy in cots + [cots_own]:
        copy.wait()
    for i in range(PARTS):
        r.grad[block(i, part_rows)] = dot(eye, r.c_in[i], NT).astype(BF16)

    upper = pl.ds(0, seq)
    lower = pl.ds(seq, seq)

    def put(count, base):
        return [
            local(
                8 + q,
                stage.at[pl.ds(2 * LANES * q, count)],
                r.parts.at[q // 2, q % 2, pl.ds(base, count)],
            )
            for q in range(PARTS)
        ]

    def put_block(i):
        return put(2 * LANES, pl.multiple_of(i * 2 * LANES, 2 * LANES))

    def feed_forward(i, tiles):
        two, count = lax.rem(i, 2), LANES * len(tiles)
        up, down = r.w_up_in[two, :, :count], r.w_down_in[two, :, :count]
        at = [pl.ds(pl.multiple_of(tile * LANES, LANES), LANES) for tile in tiles]
        bias = jnp.concatenate([r.up_bias[:, lanes] for lanes in at], axis=1)
        hidden, cot = r.h[...], r.grad[...]
        act, slope = gelu_both(dot(hidden, up, NN) + bias)
        act = act.astype(BF16)
        grad_up = (dot(cot, down, NN) * slope).astype(BF16)
        r.acc[upper, :width] += dot(act, down, NT)
        r.acc[lower, :width] += dot(grad_up, up, NT)
        total = column_sum(grad_up.astype(F32))
        for q, lanes in enumerate(at):
            vec[0:1, lanes] = total[:, LANES * q : LANES * (q + 1)]
        return dot(act, cot, TN).astype(BF16), dot(grad_up, hidden, TN).astype(BF16)

    def ff_block(i, carry):
        for copy in weights(i, main_tiles(i)):
            copy.wait()

        @pl.when(i + 1 < main)
        def _():
            for copy in weights(i + 1, main_tiles(i + 1)):
                copy.start()

        @pl.when(i + 1 == main)
        def _():
            for copy in weights(main, left_tiles):
                copy.start()

        values = feed_forward(i, main_tiles(i))

        @pl.when(i > 1)
        def _():
            for copy in put_block(i - 1):
                copy.wait()

        for j, value in enumerate(values):
            for q in range(PARTS):
                stage[LANES * (2 * q + j) : LANES * (2 * q + j + 1)] = value[
                    LANES * q : LANES * (q + 1)
                ]
        for copy in put_block(i):
            copy.start()
        return carry

    ff_block(0, 0)
    for copy in put_block(0):
        copy.wait()
    reducer.step(jnp.int32(0))

    def ff_step(s, carry):
        lax.fori_loop(2 * s - 1, 2 * s + 1, ff_block, 0)
        reducer.step(s)
        return carry

    ff_steps = main // 2
    lax.fori_loop(1, ff_steps, ff_step, 0)
    lax.fori_loop(main - 1, main, ff_block, 0)
    for copy in weights(main, left_tiles):
        copy.wait()
    values = feed_forward(main, left_tiles)
    for copy in put_block(main - 1):
        copy.wait()
    for j, value in enumerate(values):
        tiles = [value[LANES * q : LANES * (q + 1)] for q in range(PARTS - 1)]
        for q, pieces in enumerate(leftover_rows(tiles)):
            at = 2 * LANES * q + left * j
            for piece in pieces:
                stage[at : at + piece.shape[0]] = piece
                at += piece.shape[0]
    put_left = put(2 * left, 2 * LANES * main)
    for copy in put_left:
        copy.start()
    reducer.step(jnp.int32(ff_steps))
    done = ff_steps + 1
    for copy in put_left:
        copy.wait()

    def add_vector(index, value):
        vec[index : index + 1, :width] = vec[index : index + 1, :width] + value

    def middle_rows(i, carry):
        rows = block(i, part_rows)
        after = r.rows[rows]
        result = r.acc[rows, :width] + after + bias_down
        r.x_in[i] = turned(eye, result.astype(BF16)).astype(BF16)
        normed, inverse = norm_rows(after)
        grad = r.acc[pl.ds(pl.multiple_of(seq + i * part_rows, part_rows), part_rows), :width]
        cot = r.grad[rows].astype(F32)
        add_vector(3, column_sum(grad * normed))
        add_vector(4, column_sum(grad))
        add_vector(5, column_sum(cot))
        grad_after = cot + norm_rows_back(grad * gain2, normed, inverse)
        r.rows[rows] = grad_after
        r.grad[rows] = grad_after.astype(BF16)
        return carry

    lax.fori_loop(0, PARTS, middle_rows, 0)
    four = 4 * HD
    early = []
    for quarter in range(PARTS):
        start = feat * quarter // LANES * LANES
        offset = feat * quarter - start
        product = dot(r.m[:, start : start + 384], r.grad[...], TN)
        for p in range(2):
            at = four * quarter + 2 * HD * p
            first = offset + 2 * HD * p
            stage[at : at + 2 * HD] = product[first : first + 2 * HD].astype(BF16)
        r.acc[HD * quarter : HD * (quarter + 1), :width] = product[
            offset + four : offset + four + HD
        ]
        early.append(
            local(
                8 + quarter,
                stage.at[pl.ds(four * quarter, four)],
                r.parts.at[quarter // 2, quarter % 2, pl.ds(2 * ff, four)],
            )
        )
        early[-1].start()
    r.g[:, :width] = dot(r.grad[...], r.square[0], NT).astype(BF16)
    for copy in early:
        copy.wait()
    w_query = local(4, r.w_qkv.at[0], r.square.at[0])
    w_query.start()
    reducer.step(jnp.int32(done))
    done += 1
    outs, outs_own = spread(2, r.x_in, r.output)

    def head_step(s, carry):
        def one(h, carry):
            head_back(h, head_at(h), r.q, r.k, r.v, r.g, r.bias)
            return carry

        lax.fori_loop(s * group, (s + 1) * group, one, 0)
        reducer.step(done + s)
        return carry

    lax.fori_loop(0, heads // group, head_step, 0)
    done += heads // group

    def first_again(i, carry):
        rows = block(i, part_rows)
        normed, _ = norm_rows(r.x[rows].astype(F32))
        r.h[rows] = (normed * gain1 + bias1).astype(BF16)
        return carry

    lax.fori_loop(0, PARTS, first_again, 0)
    sizes = (width - 2 * feat - four, 2 * feat)
    bases = (2 * ff + four, 2 * ff + width - 2 * feat)

    def tail_put(turn):
        pair, quarter = turn // PARTS, turn % PARTS
        return local(
            8 + turn % 2,
            stage.at[pl.ds(2 * feat * (turn % 2), sizes[pair])],
            r.parts.at[quarter // 2, quarter % 2, pl.ds(bases[pair], sizes[pair])],
        )

    for turn in range(2 * PARTS):
        pair, quarter = turn // PARTS, turn % PARTS
        start = feat * quarter // LANES * LANES
        offset = feat * quarter - start
        units = [] if pair else [r.acc[HD * quarter : HD * (quarter + 1), :width]]
        for left_ref, right_ref in ((r.k, r.h), (r.v, r.h)) if pair else ((r.q, r.h),):
            product = dot(left_ref[:, start : start + 384], right_ref[...], TN)
            units += [product[offset + HD * u : offset + HD * (u + 1)] for u in range(5)]
        if turn >= 2 and turn % PARTS >= 2:
            tail_put(turn - 2).wait()
        for p in range(len(units) // 2):
            at = 2 * feat * (turn % 2) + 2 * HD * p
            stage[at : at + 2 * HD] = jnp.concatenate(units[2 * p : 2 * p + 2], axis=0).astype(
                BF16
            )
        tail_put(turn).start()
        if turn % PARTS == PARTS - 1:
            tail_put(turn - 1).wait()
            tail_put(turn).wait()
            reducer.step(jnp.int32(done))
            done += 1
    w_value = local(3, r.w_qkv.at[2], r.square.at[2])
    w_value.start()
    w_query.wait()
    r.acc[upper, :width] = dot(r.q[:, :width], r.square[0], NT)
    r.acc[upper, :width] += dot(r.k[:, :width], r.square[1], NT)
    reducer.step(jnp.int32(done))
    done += 1
    w_value.wait()
    r.acc[upper, :width] += dot(r.v[:, :width], r.square[2], NT)

    def last_norm(i, carry):
        rows = block(i, part_rows)
        normed, inverse = norm_rows(r.x[rows].astype(F32))
        grad = r.acc[rows, :width]
        add_vector(1, column_sum(grad * normed))
        add_vector(2, column_sum(grad))
        back = r.rows[rows] + norm_rows_back(grad * gain1, normed, inverse)
        r.c_in[i] = turned(eye, back.astype(BF16)).astype(BF16)
        return carry

    lax.fori_loop(0, PARTS, last_norm, 0)

    steps = reducer.rounds + 11
    grads, grads_own = spread(3, r.c_in, r.input_grad)
    turn = 32 * narrow
    lane = lax.broadcasted_iota(jnp.int32, (1, LANES), 1)

    def mix(tile, mask, value):
        lanes = pl.ds(pl.multiple_of(tile * LANES, LANES), LANES)
        r.acc[:, lanes] = jnp.where(mask, value, r.acc[:, lanes])

    def settle(j):
        base = pl.multiple_of(j * 2 * LANES, 2 * LANES)
        place = pl.multiple_of(turn + j * LANES, 32)
        get = local(4, r.total.at[pl.ds(base, 2 * LANES)], stage.at[pl.ds(0, 2 * LANES)])
        get.start()
        get.wait()
        give = local(5, stage.at[pl.ds(0, LANES)], r.down.at[pl.ds(place, LANES)])
        give.start()
        value = pltpu.roll(turned(eye, stage[LANES : 2 * LANES]), turn, 1)
        mix(j, lane >= turn, value)
        mix(j + 1, lane < turn, value)
        give.wait()

    def settle_left():
        get = local(4, r.total.at[pl.ds(2 * LANES * main, 2 * left)], stage.at[pl.ds(0, 2 * left)])
        get.start()
        get.wait()
        gives = []
        for piece in range(left // 32):
            place = lax.rem(turn + main * LANES + 32 * piece, ff)
            gives.append(
                local(
                    8 + piece,
                    stage.at[pl.ds(32 * piece, 32)],
                    r.down.at[pl.ds(pl.multiple_of(place, 32), 32)],
                )
            )
            gives[-1].start()
        value = turned(eye, stage[left : left + LANES])
        mix(main, (lane >= turn) & (lane < left), pltpu.roll(value, turn, 1))
        mix(0, lane < turn, pltpu.roll(value, lax.rem(turn + LANES - left, LANES), 1))
        r.square[0] = r.acc[:, :ff].astype(BF16)
        local(6, r.square.at[0], r.up).start()
        for copy in gives:
            copy.wait()

    def drain(t, carry):
        reducer.step(t)

        @pl.when(t == done + 3)
        def _():
            for copy in outs + [outs_own] + grads + [grads_own]:
                copy.start()

        vector_sum.step(t - done)
        at = t - done
        for i in range(2):
            pl.when(at < 3)(functools.partial(settle, 2 * at + i))
        pl.when(at == 3)(lambda: settle(6))
        pl.when(at == 5)(lambda: settle(7))
        pl.when(at == 6)(settle_left)
        return carry

    lax.fori_loop(done, steps, drain, 0)
    first = vec[0:1]
    others = vec[:, :WIDE]
    r.share[...] = pltpu.roll(others, lax.rem(WIDE - feat * narrow, WIDE), 1)
    hidden = PARTS * ff
    r.share[0:1, :ff] = pltpu.roll(first, lax.rem(hidden - ff * narrow, hidden), 1)[:, :ff]
    finish = local(7, r.share, r.vector)
    finish.start()
    for copy in outs + [outs_own] + grads + [grads_own]:
        copy.wait()
    local(6, r.square.at[0], r.up).wait()
    finish.wait()


def tokens_peer(reducer, d):
    return (reducer.at_core, reducer.at_y, reducer.at_cross)[d][1]


def softmax_parts(scores):
    expo = jnp.exp(scores - jnp.max(scores, axis=1, keepdims=True))
    return expo * (1.0 / jnp.sum(expo, axis=1, keepdims=True))


def attend_heads(pair, q_ref, k_ref, v_ref, out_ref, bias_ref):
    half = q_ref.shape[0] // 2
    results = []
    for h, start in pair:
        window = pl.ds(start, 256)
        mask = head_mask(h, start, 256)
        query = jnp.where(mask, q_ref[:, window], 0)
        keys, values = k_ref[:, window], v_ref[:, window]
        for part in range(2):
            count = (part + 1) * half
            rows = slice(part * half, count)
            scores = dot(query[rows], keys[:count], NT) * SCALE + bias_ref[rows, :count]
            probs = softmax_parts(scores).astype(BF16)
            mixed = dot(probs, values[:count], NN).astype(BF16)
            results.append((rows, window, mask, mixed))
    for rows, window, mask, mixed in results:
        out_ref[rows, window] = jnp.where(mask, mixed, out_ref[rows, window])


def head_back(h, start, q_ref, k_ref, v_ref, grad_ref, bias_ref):
    half = q_ref.shape[0] // 2
    window = pl.ds(start, 256)
    mask = head_mask(h, start, 256)
    query = jnp.where(mask, q_ref[:, window], 0)
    grad = jnp.where(mask, grad_ref[:, window], 0)
    keys, values = k_ref[:, window], v_ref[:, window]
    grads = []
    for part in range(2):
        count = (part + 1) * half
        rows = slice(part * half, count)
        scores = dot(query[rows], keys[:count], NT) * SCALE + bias_ref[rows, :count]
        grad_probs = dot(grad[rows], values[:count], NT)
        probs = softmax_parts(scores)
        inner = jnp.sum(probs * grad_probs, axis=1, keepdims=True)
        grad_scores = (probs * (grad_probs - inner) * SCALE).astype(BF16)
        gq = dot(grad_scores, keys[:count], NN).astype(BF16)
        gk = dot(grad_scores, query[rows], TN)
        gv = dot(probs.astype(BF16), grad[rows], TN)
        grads.append((gq, gk, gv))
    (gq0, gk0, gv0), (gq1, gk1, gv1) = grads
    q_ref[:half, window] = jnp.where(mask, gq0, q_ref[:half, window])
    q_ref[half:, window] = jnp.where(mask, gq1, q_ref[half:, window])
    for ref, first, second in ((k_ref, gk0, gk1), (v_ref, gv0, gv1)):
        top, bottom = (first + second[:half]).astype(BF16), second[half:].astype(BF16)
        ref[:half, window] = jnp.where(mask, top, ref[:half, window])
        ref[half:, window] = jnp.where(mask, bottom, ref[half:, window])


def whole_layer(**arrays):
    parts, width, part_rows = arrays["tokens"].shape
    seq, hidden = parts * part_rows, arrays["w_up"].shape[1]
    ff = hidden // parts
    rows = 2 * ff + width
    reducer = Reducer(128, 96, width, rows)
    scratch = reducer.scratch()
    low = lambda *shape: pltpu.VMEM(shape, BF16)
    full = lambda *shape: pltpu.VMEM(shape, F32)
    dma = lambda *shape: pltpu.SemaphoreType.DMA(shape)
    scratch.update(
        x_in=low(parts, width, part_rows),
        c_in=low(parts, width, part_rows),
        w_up_in=low(2, width, parts * LANES),
        w_down_in=low(2, width, parts * LANES),
        square=low(3, width, width),
        q=low(seq, WIDE),
        k=low(seq, WIDE),
        v=low(seq, WIDE),
        m=low(seq, WIDE),
        g=low(seq, WIDE),
        h=low(seq, width),
        grad=low(seq, width),
        x=low(seq, width),
        rows=full(seq, width),
        acc=full(width, WIDE),
        bias=low(seq, seq),
        up_bias=full(1, hidden),
        vec=full(8, hidden),
        vec_in=full(6, 8, hidden),
        share=full(8, WIDE),
        vec_send=dma(6),
        vec_recv=dma(6),
        local=dma(12),
        w_load=dma(2, 2, parts),
        spread_send=dma(4, 3),
        spread_recv=dma(4, 3),
    )
    hbm = pl.BlockSpec(memory_space=pl.ANY)
    vmem = pl.BlockSpec(memory_space=pltpu.VMEM)
    low_out = lambda *shape: jax.ShapeDtypeStruct(shape, BF16)
    outputs = dict(
        parts=low_out(2, parts // 2, rows, width),
        total=low_out(rows, width),
        down=low_out(ff, width),
        up=low_out(width, ff),
        output=low_out(parts, width, part_rows),
        input_grad=low_out(parts, width, part_rows),
        vector=jax.ShapeDtypeStruct((8, WIDE), F32),
    )
    smem = pl.BlockSpec(memory_space=pltpu.SMEM)
    names = list(arrays) + list(outputs) + list(scratch)
    results = pl.pallas_call(
        functools.partial(layer_kernel, reducer, names),
        out_shape=tuple(outputs.values()),
        in_specs=[hbm] * 6 + [smem] + [vmem] * (len(arrays) - 7),
        out_specs=[hbm] * len(outputs),
        scratch_shapes=list(scratch.values()),
        compiler_params=pltpu.CompilerParams(
            collective_id=0, has_side_effects=True, vmem_limit_bytes=VMEM_LIMIT
        ),
        name="whole_layer",
    )(*arrays.values())
    return types.SimpleNamespace(**dict(zip(outputs, results)))


def finish_kernel(names, *refs):
    r = types.SimpleNamespace(**dict(zip(names, refs)))
    rows, step = r.down.shape[0], 112
    feat = r.out.shape[0]

    def copy(index, source, target):
        return pltpu.make_async_copy(source, target, r.moves.at[index])

    loads = [
        copy(0, r.down, r.down_in),
        copy(1, r.up, r.up_in),
        copy(2, r.total.at[pl.ds(r.total.shape[0] - rows, rows)], r.rest_in),
        copy(3, r.grad, r.grad_in),
    ]
    plain = copy(4, r.output, r.output_in)
    for move in loads + [plain]:
        move.start()
    stores = []

    def store(source, target):
        stores.append(copy(5 + len(stores), source, target))
        stores[-1].start()

    r.up_bias_to[...] = r.vector[0, :rows]
    for index, target in enumerate((r.gain1, r.bias1, r.gain2, r.bias2, r.down_bias)):
        target[...] = r.vector[index + 1, :feat]
    wides = ((r.down_in, r.down_wide, r.down_to), (r.up_in, r.up_wide, r.up_to))
    for load, (source, wide, target) in zip(loads, wides):
        load.wait()
        for at in range(0, rows, step):
            wide[at : at + step] = source[at : at + step].astype(F32)
            if (at // step) % 2:
                area = pl.ds(at - step, 2 * step)
                store(wide.at[area], target.at[area])
    loads[2].wait()
    sent = 0
    for at in range(0, rows, step):
        r.rest_wide[at : at + step] = r.rest_in[at : at + step].astype(F32)
        while sent < rows and at + step >= sent + feat:
            area = pl.ds(sent, feat)
            target = r.out if sent == 0 else r.qkv.at[pl.ds(sent - feat, feat)]
            store(r.rest_wide.at[area], target)
            sent += feat
    loads[3].wait()
    for i in range(r.grad_in.shape[0]):
        r.grad_wide[i] = r.grad_in[i].astype(F32)
        store(r.grad_wide.at[i], r.grad_to.at[i])
    plain.wait()
    store(r.output_in, r.result)
    for move in stores:
        move.wait()


def finish(**arrays):
    shape = {name: array.shape for name, array in arrays.items()}
    rows, width = shape["down"]
    feat = width // PARTS
    wide = lambda *size: jax.ShapeDtypeStruct(size, F32)
    outputs = dict(
        result=jax.ShapeDtypeStruct(shape["output"], BF16),
        grad_to=wide(*shape["grad"]),
        qkv=wide(3 * feat, width),
        out=wide(feat, width),
        up_to=wide(*shape["up"]),
        down_to=wide(rows, width),
        gain1=wide(feat),
        bias1=wide(feat),
        gain2=wide(feat),
        bias2=wide(feat),
        up_bias_to=wide(rows),
        down_bias=wide(feat),
    )
    kept = lambda name: pltpu.VMEM(shape[name], arrays[name].dtype)
    square = lambda dtype: pltpu.VMEM((rows, width), dtype)
    scratch = dict(
        down_in=kept("down"),
        up_in=kept("up"),
        rest_in=square(arrays["total"].dtype),
        grad_in=kept("grad"),
        output_in=kept("output"),
        down_wide=square(F32),
        up_wide=square(F32),
        rest_wide=square(F32),
        grad_wide=pltpu.VMEM(shape["grad"], F32),
        moves=pltpu.SemaphoreType.DMA((32,)),
    )
    hbm = pl.BlockSpec(memory_space=pl.ANY)
    vmem = pl.BlockSpec(memory_space=pltpu.VMEM)
    names = list(arrays) + list(outputs) + list(scratch)
    results = pl.pallas_call(
        functools.partial(finish_kernel, names),
        out_shape=tuple(outputs.values()),
        in_specs=[hbm] * (len(arrays) - 1) + [vmem],
        out_specs=[hbm] * 6 + [vmem] * 6,
        scratch_shapes=list(scratch.values()),
        compiler_params=pltpu.CompilerParams(vmem_limit_bytes=VMEM_LIMIT),
        name="finish",
    )(*arrays.values())
    return types.SimpleNamespace(**dict(zip(outputs, results)))


def on_device(
    wide,
    tokens,
    lengths,
    norm1_gain,
    norm1_bias,
    w_qkv,
    w_out,
    norm2_gain,
    norm2_bias,
    w_up,
    bias_up,
    w_down,
    bias_down,
    cotangent,
):
    width = w_out.shape[0]
    feat = width // tokens.shape[0]
    got = whole_layer(
        tokens=tokens.transpose(0, 2, 1),
        cot=cotangent.transpose(0, 2, 1),
        w_qkv=w_qkv.transpose(1, 0, 2),
        w_out=w_out,
        w_up=w_up,
        w_down=w_down.T,
        lengths=lengths,
        gain1=norm1_gain,
        bias1=norm1_bias,
        gain2=norm2_gain,
        bias2=norm2_bias,
        bias_up=bias_up,
        bias_down=bias_down,
    )
    if wide > BLOCK:
        groups = [list(range(i, wide, BLOCK)) for i in range(BLOCK)]
        got.total, got.down, got.up, got.vector = (
            lax.psum(a.astype(F32), "wide", axis_index_groups=groups)
            for a in (got.total, got.down, got.up, got.vector)
        )
    last = finish(
        output=got.output,
        grad=got.input_grad,
        total=got.total,
        down=got.down,
        up=got.up,
        vector=got.vector,
    )
    return (
        last.result.transpose(0, 2, 1),
        last.grad_to.transpose(0, 2, 1),
        last.gain1,
        last.bias1,
        last.qkv.reshape(3, feat, width).transpose(2, 0, 1),
        last.out,
        last.gain2,
        last.bias2,
        last.up_to,
        last.up_bias_to,
        last.down_to,
        last.down_bias,
    )


def solution(mesh):
    rows = P("wide", "narrow", None)
    in_specs = (rows, P("wide")) + (P(),) * 10 + (rows,)
    out_specs = (
        rows,
        rows,
        P("narrow"),
        P("narrow"),
        P(None, None, "narrow"),
        P("narrow", None),
        P("narrow"),
        P("narrow"),
        P(None, "narrow"),
        P("narrow"),
        P("narrow", None),
        P("narrow"),
    )
    return jax.shard_map(
        functools.partial(on_device, mesh.shape["wide"]),
        mesh=mesh,
        in_specs=in_specs,
        out_specs=out_specs,
        check_vma=False,
    )
```

```python
import functools
import types

import jax
import jax.numpy as jnp
from jax import lax
from jax.experimental import pallas as pl
from jax.experimental.pallas import tpu as pltpu
from jax.sharding import PartitionSpec as P

HD = 56
SCALE = HD**-0.5
F32, BF16 = jnp.float32, jnp.bfloat16
MESH = pl.DeviceIdType.MESH
VMEM_LIMIT = 62 * 1024 * 1024
LINE, PAIR = 4, 2
BLOCK = LINE * PAIR
SLOTS = 4
CORE, CY, CA, CB, CC, CX, AX, AY, A1, A2, A3, AG, GATHER = range(13)
CHANNELS = GATHER + 6


def dot(a, b, dims):
    return lax.dot_general(a, b, (dims, ((), ())), preferred_element_type=F32)


NN, NT, TN = ((1,), (0,)), ((1,), (1,)), ((0,), (0,))


def head_mask(h, start, size):
    lane = start + lax.broadcasted_iota(jnp.int32, (1, size), 1)
    return (lane >= h * HD) & (lane < h * HD + HD)


class Reducer:
    hops = 9

    def __init__(self, rows_c, rows_a, width, total):
        self.rounds = total // (rows_c + rows_a)
        self.states, self.states_a = 10, 8
        self.rows_c, self.rows_a, self.width = rows_c, rows_a, width
        self.rows = rows_c + rows_a
        self.shard, self.half = rows_c // LINE, rows_a // 2

    def scratch(self):
        c, a, q, h, d = self.rows_c, self.rows_a, self.shard, self.half, self.width
        buffers = dict(
            own=(2, self.rows, d),
            core_in=(2, 2, self.rows, d),
            cy_out=(2, c, d),
            cy_in=(SLOTS, c, d),
            c_state=(self.states, c, d),
            ca_in=(SLOTS, 3 * q, d),
            cb_in=(SLOTS, 2 * q, d),
            cc_in=(SLOTS, q, d),
            cx_in=(SLOTS, q, d),
            ax_out=(2, 2, h, d),
            ax_keep=(2, 2, h, d),
            ax_in=(SLOTS, 2, h, d),
            ay_out=(2, h, d),
            ay_in=(SLOTS, h, d),
            a_sum=(4, h, d),
            a1_in=(SLOTS, h, d),
            a2_in=(SLOTS, h, d),
            a_state=(self.states_a, 2, h, d),
        )
        result = {name: pltpu.VMEM(shape, BF16) for name, shape in buffers.items()}
        result.update(
            net_send=pltpu.SemaphoreType.DMA((CHANNELS, SLOTS)),
            net_recv=pltpu.SemaphoreType.DMA((CHANNELS, SLOTS)),
            load=pltpu.SemaphoreType.DMA((2,)),
            c_store=pltpu.SemaphoreType.DMA((2,)),
            a_store=pltpu.SemaphoreType.DMA((2,)),
        )
        return result

    def bind(self, part_ref, out_ref, refs):
        self.part_ref, self.out_ref, self.refs = part_ref, out_ref, refs
        wide, narrow = lax.axis_index("wide"), lax.axis_index("narrow")
        self.wide, self.narrow = wide, narrow
        self.z, self.x = lax.rem(wide, BLOCK) // PAIR, lax.rem(wide, PAIR)
        self.y, self.core = narrow // 2, lax.rem(narrow, 2)
        flip = lambda index, bit: index + 1 - 2 * bit
        self.at_core = (wide, flip(narrow, self.core))
        self.at_y = (wide, narrow + 2 - 4 * self.y)
        self.at_cross = (wide, flip(narrow, self.core) + 2 - 4 * self.y)
        self.at_x = (flip(wide, self.x), narrow)
        self.at_up = (wide + PAIR, narrow)
        self.at_down = (wide - PAIR, narrow)

    def barrier(self):
        z = self.z
        barrier = pltpu.get_barrier_semaphore()

        def greet(target):
            pl.semaphore_signal(barrier, inc=1, device_id=target, device_id_type=MESH)

        for target in (self.at_core, self.at_y, self.at_cross, self.at_x):
            greet(target)
        pl.when(z < LINE - 1)(lambda: greet(self.at_up))
        pl.when(z > 0)(lambda: greet(self.at_down))
        edge = (z == 0) | (z == LINE - 1)
        pl.when(edge)(lambda: pl.semaphore_wait(barrier, 5))
        pl.when(~edge)(lambda: pl.semaphore_wait(barrier, 6))

    def copy(self, channel, k, source, target, device):
        slot = lax.rem(k, SLOTS)
        return pltpu.make_async_remote_copy(
            src_ref=source,
            dst_ref=target,
            send_sem=self.refs.net_send.at[channel, slot],
            recv_sem=self.refs.net_recv.at[channel, slot],
            device_id=device,
            device_id_type=MESH,
        )


    def load(self, k):
        r = self.refs
        return pltpu.make_async_copy(
            self.part_ref.at[:, self.core, pl.ds(k * self.rows, self.rows)],
            r.own,
            r.load.at[lax.rem(k, 2)],
        )

    def core_hop(self, k):
        return self.copy(
            CORE,
            k,
            self.part_ref.at[:, 1 - self.core, pl.ds(k * self.rows, self.rows)],
            self.refs.core_in.at[lax.rem(k, 2)],
            self.at_core,
        )

    def slotted(self, channel, k, source, device):
        r = self.refs
        arrivals = {CY: r.cy_in, CA: r.ca_in, CB: r.cb_in, CC: r.cc_in, CX: r.cx_in}
        arrivals.update({AX: r.ax_in, AY: r.ay_in, A1: r.a1_in, A2: r.a2_in})
        return self.copy(channel, k, source, arrivals[channel].at[lax.rem(k, SLOTS)], device)

    def c_rows(self, k, first, count):
        return self.refs.c_state.at[
            lax.rem(k, self.states), pl.ds(pl.multiple_of(first * self.shard, self.shard), count * self.shard)
        ]

    def line_hops(self, k):
        z, up, down = self.z, self.at_up, self.at_down
        hops = []
        for name, count, up_from in ((CA, 3, 0), (CB, 2, 1), (CC, 1, 2)):
            down_from = LINE - 1 - up_from
            hops.append(
                (
                    name,
                    [
                        (z == up_from, self.slotted(name, k, self.c_rows(k, LINE - count, count), up)),
                        (z == down_from, self.slotted(name, k, self.c_rows(k, 0, count), down)),
                    ],
                    [(z == up_from + 1, LINE - count), (z == down_from - 1, 0)],
                    count,
                )
            )
        return hops

    def gather_hops(self, k, distance):
        z = self.z
        channel = GATHER + 2 * distance
        low, high = jnp.maximum(z - distance, 0), jnp.minimum(z + distance, LINE - 1)
        return [
            (
                (z >= distance) & (z < LINE - 1),
                self.copy(channel, k, self.c_rows(k, low, 1), self.c_rows(k, low, 1), self.at_up),
                z >= distance + 1,
            ),
            (
                (z <= LINE - 1 - distance) & (z > 0),
                self.copy(channel + 1, k, self.c_rows(k, high, 1), self.c_rows(k, high, 1), self.at_down),
                z <= LINE - 2 - distance,
            ),
        ]

    def sum_hops(self, k):
        z, slot = self.z, lax.rem(k, 4)
        own = self.refs.a_sum.at[slot]
        final = self.refs.a_state.at[lax.rem(k, self.states_a), self.x]
        return {
            A1: [
                (z == 0, self.slotted(A1, k, own, self.at_up)),
                (z == LINE - 1, self.slotted(A1, k, own, self.at_down)),
            ],
            A2: [
                (z == 1, self.slotted(A2, k, own, self.at_up)),
                (z == 2, self.slotted(A2, k, own, self.at_down)),
            ],
            A3: [
                (z == 1, self.copy(A3, k, final, final, self.at_down)),
                (z == 2, self.copy(A3, k, final, final, self.at_up)),
            ],
        }

    def store(self, k):
        r, slot, two = self.refs, lax.rem(k, self.states), lax.rem(k, 2)
        base = k * self.rows
        yield pltpu.make_async_copy(
            r.c_state.at[slot], self.out_ref.at[pl.ds(base, self.rows_c)], r.c_store.at[two]
        )

    def store_a(self, k):
        r, slot, two = self.refs, lax.rem(k, self.states_a), lax.rem(k, 2)
        base = k * self.rows + self.rows_c
        for i in range(2):
            yield pltpu.make_async_copy(
                r.a_state.at[slot, i],
                self.out_ref.at[pl.ds(base + i * self.half, self.half)],
                r.a_store.at[two],
            )

    def step(self, t):
        r, c, h, q = self.refs, self.rows_c, self.half, self.shard
        x, y, z = self.x, self.y, self.z

        def stage(delay, body):
            k = t - delay
            pl.when((k >= 0) & (k < self.rounds))(lambda: body(k))

        def start_if(pairs):
            for condition, copy in pairs:
                pl.when(condition)(copy.start)

        def send_wait_if(pairs):
            for condition, copy in pairs:
                pl.when(condition)(copy.wait_send)

        def begin(k):
            self.core_hop(k).start()
            pl.when(k == 0)(self.load(k).start)


        def after_core(k):
            two, four = lax.rem(k, 2), lax.rem(k, SLOTS)
            copy = self.core_hop(k)
            copy.wait()
            self.load(k).wait()
            total = lambda i, rows: r.own[i, rows] + r.core_in[two, i, rows]
            everything = pl.ds(0, c)
            r.cy_out[two] = total(1 - y, everything)
            self.cy_hop(k).start()
            for i in range(2):
                rows = pl.ds(pl.multiple_of(c + (1 - x) * h, 16), h)
                r.ax_out[two, i] = total(i, rows)
            self.ax_hop(k).start()
            r.c_state[lax.rem(k, self.states), :] = total(y, everything)
            for i in range(2):
                rows = pl.ds(pl.multiple_of(c + x * h, 16), h)
                r.ax_keep[two, i] = total(i, rows)
            pl.when(k + 1 < self.rounds)(lambda: self.load(k + 1).start())

        stage(1, after_core)
        stage(0, begin)

        def second(k):
            two, four, slot = lax.rem(k, 2), lax.rem(k, SLOTS), lax.rem(k, self.states)
            self.cy_hop(k).wait()
            r.c_state[slot] = r.c_state[slot] + r.cy_in[four]
            start_if(self.line_hops(k)[0][1])
            self.ax_hop(k).wait()
            r.ay_out[two] = r.ax_keep[two, 1 - y] + r.ax_in[four, 1 - y]
            self.ay_hop(k).start()
            r.a_sum[lax.rem(k, 4)] = r.ax_keep[two, y] + r.ax_in[four, y]

        stage(2, second)

        def line_step(k, hop):
            name, sends, receives, count = self.line_hops(k)[hop]
            four = lax.rem(k, SLOTS)
            send_wait_if(sends)
            for condition, first in receives:

                @pl.when(condition)
                def _(first=first):
                    sends[0][1].wait_recv()
                    rows = self.c_rows(k, first, count)
                    arrived = (r.ca_in, r.cb_in, r.cc_in)[hop]
                    rows[...] = rows[...] + arrived[four]

            if hop < 2:
                start_if(self.line_hops(k)[hop + 1][1])

        def third(k):
            line_step(k, 0)
            four = lax.rem(k, SLOTS)
            self.ay_hop(k).wait()
            r.a_sum[lax.rem(k, 4)] = r.a_sum[lax.rem(k, 4)] + r.ay_in[four]
            start_if(self.sum_hops(k)[A1])

        stage(3, third)

        def fourth(k):
            line_step(k, 1)
            four, slot = lax.rem(k, SLOTS), lax.rem(k, 4)
            hops = self.sum_hops(k)
            send_wait_if(hops[A1])

            @pl.when((z > 0) & (z < LINE - 1))
            def _():
                hops[A1][0][1].wait_recv()
                r.a_sum[slot] = r.a_sum[slot] + r.a1_in[four]

            start_if(hops[A2])

        stage(4, fourth)

        def fifth(k):
            line_step(k, 2)
            self.cx_hop(k).start()
            four, slot = lax.rem(k, SLOTS), lax.rem(k, 4)
            hops = self.sum_hops(k)
            send_wait_if(hops[A2])

            @pl.when((z > 0) & (z < LINE - 1))
            def _():
                hops[A2][0][1].wait_recv()
                r.a_state[lax.rem(k, self.states_a), x] = r.a_sum[slot] + r.a2_in[four]

            start_if(hops[A3])

        stage(5, fifth)

        def sixth(k):
            four = lax.rem(k, SLOTS)
            hops = self.sum_hops(k)
            send_wait_if(hops[A3])
            pl.when((z == 0) | (z == LINE - 1))(lambda: hops[A3][0][1].wait_recv())
            self.ag_hop(k).start()
            self.cx_hop(k).wait()
            rows = self.c_rows(k, z, 1)
            rows[...] = rows[...] + r.cx_in[four]
            for sends, copy, _ in self.gather_hops(k, 0):
                pl.when(sends)(copy.start)

        stage(6, sixth)

        def gather_step(k, distance):
            for sends, copy, receives in self.gather_hops(k, distance):
                pl.when(sends)(copy.wait_send)
                pl.when(receives)(copy.wait_recv)
            if distance < 2:
                for sends, copy, _ in self.gather_hops(k, distance + 1):
                    pl.when(sends)(copy.start)

        def seventh(k):
            gather_step(k, 0)
            self.ag_hop(k).wait()
            for copy in self.store_a(k):
                copy.start()

        stage(7, seventh)

        def eighth(k):
            gather_step(k, 1)
            for copy in self.store_a(k):
                copy.wait()

        stage(8, eighth)

        def ninth(k):
            gather_step(k, 2)
            for copy in self.store(k):
                copy.start()

        stage(9, ninth)

        def tenth(k):
            for copy in self.store(k):
                copy.wait()

        stage(10, tenth)

    def cy_hop(self, k):
        return self.slotted(CY, k, self.refs.cy_out.at[lax.rem(k, 2)], self.at_y)

    def ax_hop(self, k):
        return self.slotted(AX, k, self.refs.ax_out.at[lax.rem(k, 2)], self.at_x)

    def ay_hop(self, k):
        return self.slotted(AY, k, self.refs.ay_out.at[lax.rem(k, 2)], self.at_y)

    def cx_hop(self, k):
        return self.slotted(CX, k, self.c_rows(k, self.z, 1), self.at_x)

    def ag_hop(self, k):
        final = self.refs.a_state.at[lax.rem(k, self.states_a), self.x]
        return self.copy(AG, k, final, final, self.at_x)


class VectorSum:
    def __init__(self, reducer, value, arrived, send, recv):
        self.value, self.arrived, self.send, self.recv = value, arrived, send, recv
        self.net = reducer

    def hop(self, index, device):
        return pltpu.make_async_remote_copy(
            src_ref=self.value,
            dst_ref=self.arrived.at[index],
            send_sem=self.send.at[index],
            recv_sem=self.recv.at[index],
            device_id=device,
            device_id_type=MESH,
        )

    def exchange(self, index):
        return self.hop(index, (self.net.at_core, self.net.at_y, self.net.at_x)[index])

    def step(self, at):
        z, value, arrived = self.net.z, self.value, self.arrived
        middle = (z > 0) & (z < LINE - 1)
        sends = {
            3: ((z == 0, self.net.at_up), (z == LINE - 1, self.net.at_down)),
            4: ((z == 1, self.net.at_up), (z == 2, self.net.at_down)),
            5: ((z == 1, self.net.at_down), (z == 2, self.net.at_up)),
        }

        def start(index):
            for condition, device in sends[index]:
                pl.when(condition)(self.hop(index, device).start)

        def finish(index, receives, add):
            for condition, device in sends[index]:
                pl.when(condition)(self.hop(index, device).wait_send)

            @pl.when(receives)
            def _():
                self.hop(index, sends[index][0][1]).wait_recv()
                value[...] = arrived[index] + value[...] if add else arrived[index]

        def first():
            self.exchange(0).start()

        def pair(index):
            self.exchange(index).wait()
            value[...] = value[...] + arrived[index]
            if index < 2:
                self.exchange(index + 1).start()
            else:
                start(3)

        def outer():
            finish(3, middle, True)
            start(4)

        def inner():
            finish(4, middle, True)
            start(5)

        pl.when(at == 0)(first)
        for index in range(3):
            pl.when(at == index + 1)(functools.partial(pair, index))
        pl.when(at == 4)(outer)
        pl.when(at == 5)(inner)
        pl.when(at == 6)(lambda: finish(5, (z == 0) | (z == LINE - 1), False))


LANES = 128
PARTS = 4
WIDE = 1152


def gelu_both(u):
    c0, c1 = 0.7978845608028654, 0.044715
    square = u * u
    t = jnp.tanh(c0 * u * (1.0 + c1 * square))
    half = 0.5 + 0.5 * t
    slope = half + (0.5 * c0) * u * (1.0 - t * t) * (1.0 + (3.0 * c1) * square)
    return u * half, slope


def norm_rows(values):
    centred = values - jnp.mean(values, axis=-1, keepdims=True)
    inverse = lax.rsqrt(jnp.mean(centred * centred, axis=-1, keepdims=True) + 1e-05)
    return centred * inverse, inverse


def norm_rows_back(grad_hat, normed, inverse):
    mean_grad = jnp.mean(grad_hat, axis=-1, keepdims=True)
    mean_cross = jnp.mean(grad_hat * normed, axis=-1, keepdims=True)
    return inverse * (grad_hat - mean_grad - normed * mean_cross)


def column_sum(values):
    return jnp.sum(values, axis=0, keepdims=True)


def block(i, count):
    return pl.ds(pl.multiple_of(i * count, count), count)


def identity(size):
    row = lax.broadcasted_iota(jnp.int32, (size, size), 0)
    column = lax.broadcasted_iota(jnp.int32, (size, size), 1)
    return jnp.where(row == column, 1.0, 0.0).astype(BF16)


def turned(eye, rows):
    width = rows.shape[1]
    pieces = []
    for at in range(0, width, LANES):
        size = min(LANES, width - at)
        pieces.append(dot(eye[:size, :size], rows[:, at : at + size], NT))
    return jnp.concatenate(pieces, axis=0)


def leftover_rows(tiles):
    first, second, third = tiles
    return [
        [first[:96]],
        [second[:64], first[96:]],
        [third[:32], second[64:]],
        [third[32:]],
    ]


def layer_kernel(reducer, names, *refs):
    r = types.SimpleNamespace(**dict(zip(names, refs)))
    width, part_rows = r.tokens.shape[1:]
    seq = PARTS * part_rows
    feat, ff = width // PARTS, r.w_up.shape[1] // PARTS
    main = ff // LANES
    left = ff - main * LANES
    stride = (r.w_up.shape[1] // LANES - main) // (PARTS - 1)
    heads, group = width // HD, 5
    reducer.bind(r.parts, r.total, r)
    narrow, y = reducer.narrow, reducer.y
    gain1, bias1, gain2, bias2, bias_down = (
        ref[...].reshape(1, width) for ref in (r.gain1, r.bias1, r.gain2, r.bias2, r.bias_down)
    )
    eye = identity(LANES)
    vec = r.vec
    stage = r.square.at[2]
    vector_sum = VectorSum(reducer, vec, r.vec_in, r.vec_send, r.vec_recv)

    def local(index, source, target):
        return pltpu.make_async_copy(source, target, r.local.at[index])

    def spread(j, source, target):
        remote = [
            pltpu.make_async_remote_copy(
                src_ref=source.at[device[1]],
                dst_ref=target.at[narrow],
                send_sem=r.spread_send.at[j, d],
                recv_sem=r.spread_recv.at[j, d],
                device_id=device,
                device_id_type=MESH,
            )
            for d, device in enumerate((reducer.at_core, reducer.at_y, reducer.at_cross))
        ]
        return remote, local(j, source.at[narrow], target.at[narrow])

    def weights(i, tiles):
        two = lax.rem(i, 2)
        return [
            pltpu.make_async_copy(
                source.at[:, pl.ds(pl.multiple_of(tile * LANES, LANES), LANES)],
                target.at[two, :, pl.ds(q * LANES, LANES)],
                r.w_load.at[two, n, q],
            )
            for n, (source, target) in enumerate(((r.w_up, r.w_up_in), (r.w_down, r.w_down_in)))
            for q, tile in enumerate(tiles)
        ]

    main_tiles = lambda i: [i + stride * q for q in range(PARTS)]
    left_tiles = [main + stride * q for q in range(PARTS - 1)]

    squares = [local(4 + j, r.w_qkv.at[j], r.square.at[j]) for j in range(3)]
    for copy in squares:
        copy.start()
    reducer.barrier()
    tokens, tokens_own = spread(0, r.tokens, r.x_in)
    cots, cots_own = spread(1, r.cot, r.c_in)
    for copy in tokens + [tokens_own]:
        copy.start()
    cots[0].start()
    cots_own.start()
    for copy in weights(0, main_tiles(0)):
        copy.start()
    vec[...] = jnp.zeros_like(vec)
    for target in (r.q, r.k, r.v, r.m, r.g):
        target[:, width:] = jnp.zeros((seq, WIDE - width), BF16)
    r.acc[...] = jnp.zeros_like(r.acc)
    row = lax.broadcasted_iota(jnp.int32, (seq, seq), 0)
    column = lax.broadcasted_iota(jnp.int32, (seq, seq), 1)
    length = r.lengths[narrow]
    r.bias[...] = jnp.where((column <= row) & (column < length), 0.0, -1e30).astype(BF16)
    r.up_bias[...] = r.bias_up[...].reshape(r.up_bias.shape)

    def first_norm(i):
        rows = block(i, part_rows)
        x = dot(eye, r.x_in[i], NT)
        r.x[rows] = x.astype(BF16)
        normed, _ = norm_rows(x)
        r.h[rows] = (normed * gain1 + bias1).astype(BF16)

    def project(side):
        rows = block(side, seq // 2)
        for j, target in enumerate((r.q, r.k, r.v)):
            target[rows, :width] = dot(r.h[rows], r.square[j], NN).astype(BF16)

    tokens_own.wait()
    first_norm(narrow)
    tokens[0].wait()
    first_norm(tokens_peer(reducer, 0))
    for copy in squares:
        copy.wait()
    project(y)
    for d in (1, 2):
        tokens[d].wait_send()
        cots[d].start()
    for d in (1, 2):
        tokens[d].wait_recv()
        first_norm(tokens_peer(reducer, d))
    project(1 - y)
    w_out = local(4, r.w_out, r.square.at[0])
    w_out.start()

    def head_at(h):
        return pl.multiple_of(jnp.minimum(h * HD // LANES * LANES, WIDE - 256), LANES)

    def forward(i, carry):
        pair = [(h, head_at(h)) for h in (2 * i, 2 * i + 1)]
        attend_heads(pair, r.q, r.k, r.v, r.m, r.bias)
        return carry

    lax.fori_loop(0, heads // 2, forward, 0)
    w_out.wait()

    def second_norm(i, carry):
        rows = block(i, part_rows)
        after = r.x[rows].astype(F32) + dot(r.m[rows, :width], r.square[0], NN)
        r.rows[rows] = after
        normed, _ = norm_rows(after)
        r.h[rows] = (normed * gain2 + bias2).astype(BF16)
        return carry

    lax.fori_loop(0, PARTS, second_norm, 0)
    for copy in cots + [cots_own]:
        copy.wait()
    for i in range(PARTS):
        r.grad[block(i, part_rows)] = dot(eye, r.c_in[i], NT).astype(BF16)

    upper = pl.ds(0, seq)
    lower = pl.ds(seq, seq)

    def put(count, base):
        return [
            local(
                8 + q,
                stage.at[pl.ds(2 * LANES * q, count)],
                r.parts.at[q // 2, q % 2, pl.ds(base, count)],
            )
            for q in range(PARTS)
        ]

    def put_block(i):
        return put(2 * LANES, pl.multiple_of(i * 2 * LANES, 2 * LANES))

    def feed_forward(i, tiles):
        two, count = lax.rem(i, 2), LANES * len(tiles)
        up, down = r.w_up_in[two, :, :count], r.w_down_in[two, :, :count]
        at = [pl.ds(pl.multiple_of(tile * LANES, LANES), LANES) for tile in tiles]
        bias = jnp.concatenate([r.up_bias[:, lanes] for lanes in at], axis=1)
        hidden, cot = r.h[...], r.grad[...]
        act, slope = gelu_both(dot(hidden, up, NN) + bias)
        act = act.astype(BF16)
        grad_up = (dot(cot, down, NN) * slope).astype(BF16)
        r.acc[upper, :width] += dot(act, down, NT)
        r.acc[lower, :width] += dot(grad_up, up, NT)
        total = column_sum(grad_up.astype(F32))
        for q, lanes in enumerate(at):
            vec[0:1, lanes] = total[:, LANES * q : LANES * (q + 1)]
        return dot(act, cot, TN).astype(BF16), dot(grad_up, hidden, TN).astype(BF16)

    def ff_block(i, carry):
        for copy in weights(i, main_tiles(i)):
            copy.wait()

        @pl.when(i + 1 < main)
        def _():
            for copy in weights(i + 1, main_tiles(i + 1)):
                copy.start()

        @pl.when(i + 1 == main)
        def _():
            for copy in weights(main, left_tiles):
                copy.start()

        values = feed_forward(i, main_tiles(i))

        @pl.when(i > 3)
        def _():
            for copy in put_block(i - 1):
                copy.wait()

        for j, value in enumerate(values):
            for q in range(PARTS):
                stage[LANES * (2 * q + j) : LANES * (2 * q + j + 1)] = value[
                    LANES * q : LANES * (q + 1)
                ]
        for copy in put_block(i):
            copy.start()
        return carry

    ff_block(0, 0)
    for copy in put_block(0):
        copy.wait()
    reducer.step(jnp.int32(0))

    def ff_step(s, carry):
        first = jnp.where(s < 3, s, 2 * s - 3)
        last = jnp.where(s < 3, s + 1, 2 * s - 1)
        lax.fori_loop(first, last, ff_block, 0)

        @pl.when(s < 3)
        def _():
            for copy in put_block(s):
                copy.wait()

        reducer.step(s)
        return carry

    ff_steps = main // 2 + 1
    lax.fori_loop(1, ff_steps, ff_step, 0)
    lax.fori_loop(main - 1, main, ff_block, 0)
    for copy in weights(main, left_tiles):
        copy.wait()
    values = feed_forward(main, left_tiles)
    for copy in put_block(main - 1):
        copy.wait()
    for j, value in enumerate(values):
        tiles = [value[LANES * q : LANES * (q + 1)] for q in range(PARTS - 1)]
        for q, pieces in enumerate(leftover_rows(tiles)):
            at = 2 * LANES * q + left * j
            for piece in pieces:
                stage[at : at + piece.shape[0]] = piece
                at += piece.shape[0]
    put_left = put(2 * left, 2 * LANES * main)
    for copy in put_left:
        copy.start()
    reducer.step(jnp.int32(ff_steps))
    done = ff_steps + 1
    for copy in put_left:
        copy.wait()

    def add_vector(index, value):
        vec[index : index + 1, :width] = vec[index : index + 1, :width] + value

    def middle_rows(i, carry):
        rows = block(i, part_rows)
        after = r.rows[rows]
        result = r.acc[rows, :width] + after + bias_down
        r.x_in[i] = turned(eye, result.astype(BF16)).astype(BF16)
        normed, inverse = norm_rows(after)
        grad = r.acc[pl.ds(pl.multiple_of(seq + i * part_rows, part_rows), part_rows), :width]
        cot = r.grad[rows].astype(F32)
        add_vector(3, column_sum(grad * normed))
        add_vector(4, column_sum(grad))
        add_vector(5, column_sum(cot))
        grad_after = cot + norm_rows_back(grad * gain2, normed, inverse)
        r.rows[rows] = grad_after
        r.grad[rows] = grad_after.astype(BF16)
        return carry

    lax.fori_loop(0, PARTS, middle_rows, 0)
    four = 4 * HD
    early = []
    for quarter in range(PARTS):
        start = feat * quarter // LANES * LANES
        offset = feat * quarter - start
        product = dot(r.m[:, start : start + 384], r.grad[...], TN)
        for p in range(2):
            at = four * quarter + 2 * HD * p
            first = offset + 2 * HD * p
            stage[at : at + 2 * HD] = product[first : first + 2 * HD].astype(BF16)
        r.acc[HD * quarter : HD * (quarter + 1), :width] = product[
            offset + four : offset + four + HD
        ]
        early.append(
            local(
                8 + quarter,
                stage.at[pl.ds(four * quarter, four)],
                r.parts.at[quarter // 2, quarter % 2, pl.ds(2 * ff, four)],
            )
        )
        early[-1].start()
    r.g[:, :width] = dot(r.grad[...], r.square[0], NT).astype(BF16)
    for copy in early:
        copy.wait()
    w_query = local(4, r.w_qkv.at[0], r.square.at[0])
    w_query.start()
    reducer.step(jnp.int32(done))
    done += 1
    outs, outs_own = spread(2, r.x_in, r.output)

    def head_step(s, carry):
        def one(h, carry):
            head_back(h, head_at(h), r.q, r.k, r.v, r.g, r.bias)
            return carry

        lax.fori_loop(s * group, (s + 1) * group, one, 0)
        reducer.step(done + s)
        return carry

    lax.fori_loop(0, heads // group, head_step, 0)
    done += heads // group

    def first_again(i, carry):
        rows = block(i, part_rows)
        normed, _ = norm_rows(r.x[rows].astype(F32))
        r.h[rows] = (normed * gain1 + bias1).astype(BF16)
        return carry

    lax.fori_loop(0, PARTS, first_again, 0)
    sizes = (width - 2 * feat - four, 2 * feat)
    bases = (2 * ff + four, 2 * ff + width - 2 * feat)

    def tail_put(turn):
        pair, quarter = turn // PARTS, turn % PARTS
        return local(
            8 + turn % 2,
            stage.at[pl.ds(2 * feat * (turn % 2), sizes[pair])],
            r.parts.at[quarter // 2, quarter % 2, pl.ds(bases[pair], sizes[pair])],
        )

    for turn in range(2 * PARTS):
        pair, quarter = turn // PARTS, turn % PARTS
        start = feat * quarter // LANES * LANES
        offset = feat * quarter - start
        units = [] if pair else [r.acc[HD * quarter : HD * (quarter + 1), :width]]
        for left_ref, right_ref in ((r.k, r.h), (r.v, r.h)) if pair else ((r.q, r.h),):
            product = dot(left_ref[:, start : start + 384], right_ref[...], TN)
            units += [product[offset + HD * u : offset + HD * (u + 1)] for u in range(5)]
        if turn >= 2 and turn % PARTS >= 2:
            tail_put(turn - 2).wait()
        for p in range(len(units) // 2):
            at = 2 * feat * (turn % 2) + 2 * HD * p
            stage[at : at + 2 * HD] = jnp.concatenate(units[2 * p : 2 * p + 2], axis=0).astype(
                BF16
            )
        tail_put(turn).start()
        if turn % PARTS == PARTS - 1:
            tail_put(turn - 1).wait()
            tail_put(turn).wait()
            reducer.step(jnp.int32(done))
            done += 1
    w_value = local(3, r.w_qkv.at[2], r.square.at[2])
    w_value.start()
    w_query.wait()
    r.acc[upper, :width] = dot(r.q[:, :width], r.square[0], NT)
    r.acc[upper, :width] += dot(r.k[:, :width], r.square[1], NT)
    reducer.step(jnp.int32(done))
    done += 1
    w_value.wait()
    r.acc[upper, :width] += dot(r.v[:, :width], r.square[2], NT)

    def last_norm(i, carry):
        rows = block(i, part_rows)
        normed, inverse = norm_rows(r.x[rows].astype(F32))
        grad = r.acc[rows, :width]
        add_vector(1, column_sum(grad * normed))
        add_vector(2, column_sum(grad))
        back = r.rows[rows] + norm_rows_back(grad * gain1, normed, inverse)
        r.c_in[i] = turned(eye, back.astype(BF16)).astype(BF16)
        return carry

    lax.fori_loop(0, PARTS, last_norm, 0)

    steps = reducer.rounds + 11
    grads, grads_own = spread(3, r.c_in, r.input_grad)
    turn = 32 * narrow
    lane = lax.broadcasted_iota(jnp.int32, (1, LANES), 1)

    def mix(tile, mask, value):
        lanes = pl.ds(pl.multiple_of(tile * LANES, LANES), LANES)
        r.acc[:, lanes] = jnp.where(mask, value, r.acc[:, lanes])

    def settle(j):
        base = pl.multiple_of(j * 2 * LANES, 2 * LANES)
        place = pl.multiple_of(turn + j * LANES, 32)
        get = local(4, r.total.at[pl.ds(base, 2 * LANES)], stage.at[pl.ds(0, 2 * LANES)])
        get.start()
        get.wait()
        give = local(5, stage.at[pl.ds(0, LANES)], r.down.at[pl.ds(place, LANES)])
        give.start()
        value = pltpu.roll(turned(eye, stage[LANES : 2 * LANES]), turn, 1)
        mix(j, lane >= turn, value)
        mix(j + 1, lane < turn, value)
        give.wait()

    def settle_left():
        get = local(4, r.total.at[pl.ds(2 * LANES * main, 2 * left)], stage.at[pl.ds(0, 2 * left)])
        get.start()
        get.wait()
        gives = []
        for piece in range(left // 32):
            place = lax.rem(turn + main * LANES + 32 * piece, ff)
            gives.append(
                local(
                    8 + piece,
                    stage.at[pl.ds(32 * piece, 32)],
                    r.down.at[pl.ds(pl.multiple_of(place, 32), 32)],
                )
            )
            gives[-1].start()
        value = turned(eye, stage[left : left + LANES])
        mix(main, (lane >= turn) & (lane < left), pltpu.roll(value, turn, 1))
        mix(0, lane < turn, pltpu.roll(value, lax.rem(turn + LANES - left, LANES), 1))
        r.square[0] = r.acc[:, :ff].astype(BF16)
        local(6, r.square.at[0], r.up).start()
        for copy in gives:
            copy.wait()

    def drain(t, carry):
        reducer.step(t)

        @pl.when(t == done + 3)
        def _():
            for copy in outs + [outs_own] + grads + [grads_own]:
                copy.start()

        vector_sum.step(t - done)
        at = t - done
        for i in range(2):
            pl.when(at < 3)(functools.partial(settle, 2 * at + i))
        pl.when(at == 3)(lambda: settle(6))
        pl.when(at == 5)(lambda: settle(7))
        pl.when(at == 6)(settle_left)
        return carry

    lax.fori_loop(done, steps, drain, 0)
    first = vec[0:1]
    others = vec[:, :WIDE]
    r.share[...] = pltpu.roll(others, lax.rem(WIDE - feat * narrow, WIDE), 1)
    hidden = PARTS * ff
    r.share[0:1, :ff] = pltpu.roll(first, lax.rem(hidden - ff * narrow, hidden), 1)[:, :ff]
    finish = local(7, r.share, r.vector)
    finish.start()
    for copy in outs + [outs_own] + grads + [grads_own]:
        copy.wait()
    local(6, r.square.at[0], r.up).wait()
    finish.wait()


def tokens_peer(reducer, d):
    return (reducer.at_core, reducer.at_y, reducer.at_cross)[d][1]


def softmax_parts(scores):
    expo = jnp.exp(scores - jnp.max(scores, axis=1, keepdims=True))
    return expo * (1.0 / jnp.sum(expo, axis=1, keepdims=True))


def attend_heads(pair, q_ref, k_ref, v_ref, out_ref, bias_ref):
    half = q_ref.shape[0] // 2
    results = []
    for h, start in pair:
        window = pl.ds(start, 256)
        mask = head_mask(h, start, 256)
        query = jnp.where(mask, q_ref[:, window], 0)
        keys, values = k_ref[:, window], v_ref[:, window]
        for part in range(2):
            count = (part + 1) * half
            rows = slice(part * half, count)
            scores = dot(query[rows], keys[:count], NT) * SCALE + bias_ref[rows, :count]
            probs = softmax_parts(scores).astype(BF16)
            mixed = dot(probs, values[:count], NN).astype(BF16)
            results.append((rows, window, mask, mixed))
    for rows, window, mask, mixed in results:
        out_ref[rows, window] = jnp.where(mask, mixed, out_ref[rows, window])


def head_back(h, start, q_ref, k_ref, v_ref, grad_ref, bias_ref):
    half = q_ref.shape[0] // 2
    window = pl.ds(start, 256)
    mask = head_mask(h, start, 256)
    query = jnp.where(mask, q_ref[:, window], 0)
    grad = jnp.where(mask, grad_ref[:, window], 0)
    keys, values = k_ref[:, window], v_ref[:, window]
    grads = []
    for part in range(2):
        count = (part + 1) * half
        rows = slice(part * half, count)
        scores = dot(query[rows], keys[:count], NT) * SCALE + bias_ref[rows, :count]
        grad_probs = dot(grad[rows], values[:count], NT)
        probs = softmax_parts(scores)
        inner = jnp.sum(probs * grad_probs, axis=1, keepdims=True)
        grad_scores = (probs * (grad_probs - inner) * SCALE).astype(BF16)
        gq = dot(grad_scores, keys[:count], NN).astype(BF16)
        gk = dot(grad_scores, query[rows], TN)
        gv = dot(probs.astype(BF16), grad[rows], TN)
        grads.append((gq, gk, gv))
    (gq0, gk0, gv0), (gq1, gk1, gv1) = grads
    q_ref[:half, window] = jnp.where(mask, gq0, q_ref[:half, window])
    q_ref[half:, window] = jnp.where(mask, gq1, q_ref[half:, window])
    for ref, first, second in ((k_ref, gk0, gk1), (v_ref, gv0, gv1)):
        top, bottom = (first + second[:half]).astype(BF16), second[half:].astype(BF16)
        ref[:half, window] = jnp.where(mask, top, ref[:half, window])
        ref[half:, window] = jnp.where(mask, bottom, ref[half:, window])


def whole_layer(**arrays):
    parts, width, part_rows = arrays["tokens"].shape
    seq, hidden = parts * part_rows, arrays["w_up"].shape[1]
    ff = hidden // parts
    rows = 2 * ff + width
    reducer = Reducer(128, 96, width, rows)
    scratch = reducer.scratch()
    low = lambda *shape: pltpu.VMEM(shape, BF16)
    full = lambda *shape: pltpu.VMEM(shape, F32)
    dma = lambda *shape: pltpu.SemaphoreType.DMA(shape)
    scratch.update(
        x_in=low(parts, width, part_rows),
        c_in=low(parts, width, part_rows),
        w_up_in=low(2, width, parts * LANES),
        w_down_in=low(2, width, parts * LANES),
        square=low(3, width, width),
        q=low(seq, WIDE),
        k=low(seq, WIDE),
        v=low(seq, WIDE),
        m=low(seq, WIDE),
        g=low(seq, WIDE),
        h=low(seq, width),
        grad=low(seq, width),
        x=low(seq, width),
        rows=full(seq, width),
        acc=full(width, WIDE),
        bias=low(seq, seq),
        up_bias=full(1, hidden),
        vec=full(8, hidden),
        vec_in=full(6, 8, hidden),
        share=full(8, WIDE),
        vec_send=dma(6),
        vec_recv=dma(6),
        local=dma(12),
        w_load=dma(2, 2, parts),
        spread_send=dma(4, 3),
        spread_recv=dma(4, 3),
    )
    hbm = pl.BlockSpec(memory_space=pl.ANY)
    vmem = pl.BlockSpec(memory_space=pltpu.VMEM)
    low_out = lambda *shape: jax.ShapeDtypeStruct(shape, BF16)
    outputs = dict(
        parts=low_out(2, parts // 2, rows, width),
        total=low_out(rows, width),
        down=low_out(ff, width),
        up=low_out(width, ff),
        output=low_out(parts, width, part_rows),
        input_grad=low_out(parts, width, part_rows),
        vector=jax.ShapeDtypeStruct((8, WIDE), F32),
    )
    smem = pl.BlockSpec(memory_space=pltpu.SMEM)
    names = list(arrays) + list(outputs) + list(scratch)
    results = pl.pallas_call(
        functools.partial(layer_kernel, reducer, names),
        out_shape=tuple(outputs.values()),
        in_specs=[hbm] * 6 + [smem] + [vmem] * (len(arrays) - 7),
        out_specs=[hbm] * len(outputs),
        scratch_shapes=list(scratch.values()),
        compiler_params=pltpu.CompilerParams(
            collective_id=0, has_side_effects=True, vmem_limit_bytes=VMEM_LIMIT
        ),
        name="whole_layer",
    )(*arrays.values())
    return types.SimpleNamespace(**dict(zip(outputs, results)))


def finish_kernel(names, *refs):
    r = types.SimpleNamespace(**dict(zip(names, refs)))
    rows, step = r.down.shape[0], 112
    feat = r.out.shape[0]

    def copy(index, source, target):
        return pltpu.make_async_copy(source, target, r.moves.at[index])

    loads = [
        copy(0, r.down, r.down_in),
        copy(1, r.up, r.up_in),
        copy(2, r.total.at[pl.ds(r.total.shape[0] - rows, rows)], r.rest_in),
        copy(3, r.grad, r.grad_in),
    ]
    plain = copy(4, r.output, r.output_in)
    for move in loads + [plain]:
        move.start()
    stores = []

    def store(source, target):
        stores.append(copy(5 + len(stores), source, target))
        stores[-1].start()

    r.up_bias_to[...] = r.vector[0, :rows]
    for index, target in enumerate((r.gain1, r.bias1, r.gain2, r.bias2, r.down_bias)):
        target[...] = r.vector[index + 1, :feat]
    wides = ((r.down_in, r.down_wide, r.down_to), (r.up_in, r.up_wide, r.up_to))
    for load, (source, wide, target) in zip(loads, wides):
        load.wait()
        for at in range(0, rows, step):
            wide[at : at + step] = source[at : at + step].astype(F32)
            if (at // step) % 2:
                area = pl.ds(at - step, 2 * step)
                store(wide.at[area], target.at[area])
    loads[2].wait()
    sent = 0
    for at in range(0, rows, step):
        r.rest_wide[at : at + step] = r.rest_in[at : at + step].astype(F32)
        while sent < rows and at + step >= sent + feat:
            area = pl.ds(sent, feat)
            target = r.out if sent == 0 else r.qkv.at[pl.ds(sent - feat, feat)]
            store(r.rest_wide.at[area], target)
            sent += feat
    loads[3].wait()
    for i in range(r.grad_in.shape[0]):
        r.grad_wide[i] = r.grad_in[i].astype(F32)
        store(r.grad_wide.at[i], r.grad_to.at[i])
    plain.wait()
    store(r.output_in, r.result)
    for move in stores:
        move.wait()


def finish(**arrays):
    shape = {name: array.shape for name, array in arrays.items()}
    rows, width = shape["down"]
    feat = width // PARTS
    wide = lambda *size: jax.ShapeDtypeStruct(size, F32)
    outputs = dict(
        result=jax.ShapeDtypeStruct(shape["output"], BF16),
        grad_to=wide(*shape["grad"]),
        qkv=wide(3 * feat, width),
        out=wide(feat, width),
        up_to=wide(*shape["up"]),
        down_to=wide(rows, width),
        gain1=wide(feat),
        bias1=wide(feat),
        gain2=wide(feat),
        bias2=wide(feat),
        up_bias_to=wide(rows),
        down_bias=wide(feat),
    )
    kept = lambda name: pltpu.VMEM(shape[name], arrays[name].dtype)
    square = lambda dtype: pltpu.VMEM((rows, width), dtype)
    scratch = dict(
        down_in=kept("down"),
        up_in=kept("up"),
        rest_in=square(arrays["total"].dtype),
        grad_in=kept("grad"),
        output_in=kept("output"),
        down_wide=square(F32),
        up_wide=square(F32),
        rest_wide=square(F32),
        grad_wide=pltpu.VMEM(shape["grad"], F32),
        moves=pltpu.SemaphoreType.DMA((32,)),
    )
    hbm = pl.BlockSpec(memory_space=pl.ANY)
    vmem = pl.BlockSpec(memory_space=pltpu.VMEM)
    names = list(arrays) + list(outputs) + list(scratch)
    results = pl.pallas_call(
        functools.partial(finish_kernel, names),
        out_shape=tuple(outputs.values()),
        in_specs=[hbm] * (len(arrays) - 1) + [vmem],
        out_specs=[hbm] * 6 + [vmem] * 6,
        scratch_shapes=list(scratch.values()),
        compiler_params=pltpu.CompilerParams(vmem_limit_bytes=VMEM_LIMIT),
        name="finish",
    )(*arrays.values())
    return types.SimpleNamespace(**dict(zip(outputs, results)))


def on_device(
    wide,
    tokens,
    lengths,
    norm1_gain,
    norm1_bias,
    w_qkv,
    w_out,
    norm2_gain,
    norm2_bias,
    w_up,
    bias_up,
    w_down,
    bias_down,
    cotangent,
):
    width = w_out.shape[0]
    feat = width // tokens.shape[0]
    got = whole_layer(
        tokens=tokens.transpose(0, 2, 1),
        cot=cotangent.transpose(0, 2, 1),
        w_qkv=w_qkv.transpose(1, 0, 2),
        w_out=w_out,
        w_up=w_up,
        w_down=w_down.T,
        lengths=lengths,
        gain1=norm1_gain,
        bias1=norm1_bias,
        gain2=norm2_gain,
        bias2=norm2_bias,
        bias_up=bias_up,
        bias_down=bias_down,
    )
    if wide > BLOCK:
        groups = [list(range(i, wide, BLOCK)) for i in range(BLOCK)]
        got.total, got.down, got.up, got.vector = (
            lax.psum(a.astype(F32), "wide", axis_index_groups=groups)
            for a in (got.total, got.down, got.up, got.vector)
        )
    last = finish(
        output=got.output,
        grad=got.input_grad,
        total=got.total,
        down=got.down,
        up=got.up,
        vector=got.vector,
    )
    return (
        last.result.transpose(0, 2, 1),
        last.grad_to.transpose(0, 2, 1),
        last.gain1,
        last.bias1,
        last.qkv.reshape(3, feat, width).transpose(2, 0, 1),
        last.out,
        last.gain2,
        last.bias2,
        last.up_to,
        last.up_bias_to,
        last.down_to,
        last.down_bias,
    )


def solution(mesh):
    rows = P("wide", "narrow", None)
    in_specs = (rows, P("wide")) + (P(),) * 10 + (rows,)
    out_specs = (
        rows,
        rows,
        P("narrow"),
        P("narrow"),
        P(None, None, "narrow"),
        P("narrow", None),
        P("narrow"),
        P("narrow"),
        P(None, "narrow"),
        P("narrow"),
        P("narrow", None),
        P("narrow"),
    )
    return jax.shard_map(
        functools.partial(on_device, mesh.shape["wide"]),
        mesh=mesh,
        in_specs=in_specs,
        out_specs=out_specs,
        check_vma=False,
    )
```
